128 devices in a mesh: lat: 4 (over z_hi, core), lon: 32 (over z_lo, y, x).
Axes of the slice: x: 4, y: 4, z: 4 (z_hi: 2, z_lo: 2; z = z_hi * 2 + z_lo), core: 2. Of those that a mesh axis runs over, the one named last changes fastest.
Arguments:
- point_values: float32 [2, 8192, 256], P(None, ('lat', 'lon')), may hold values from -6 to 6
- theta_weights: bfloat16 [8192, 32, 256], P(('lat', 'lon')), may hold values from -1.796875 to 1.796875
- phi_weights: bfloat16 [8192, 128, 256], P(('lat', 'lon')), may hold values from -1.796875 to 1.796875
- block_counts: int32 [8192], P(('lat', 'lon')), may hold values from 0 to 256, as said below
- theta_offsets: int32 [8192], P(('lat', 'lon')), may hold values from 0 to 1024
- phi_offsets: int32 [8192], P(('lat', 'lon')), may hold values from 0 to 256
- conversion: bfloat16 [128, 4096, 2048], P(('lat', 'lon')), may hold values from -0.09375 to 0.09375
Outputs:
- coefficients: float32 [128, 2, 2048], P(('lat', 'lon'))
The draws below stay inside these ranges and needn't reach their ends.
Inputs may be any that keep to these rules, and one draw needn't show every extreme that they name: `block_counts`: within the blocks of one tile, the blocks that hold points come first; the first block of every tile holds 256 points.
All inputs are finite; a program needn't handle non-finite values.
Results may differ from the reference program's by a relative error of at most 0.004.
Values sent between devices are 32-bit elements; how exact they have to be, the bound alone decides.
A program may use at most 192 MiB of HBM per device.

```python
import math
import jax
import jax.numpy as jnp
from jax import lax

GRID_ROWS = 4096
GRID_COLS = 8192
WIN_ROWS = 32
WIN_COLS = 128
PTS = 256
BLK_DEV = 64
ROWS_DEV = 1024
COLS_DEV = 256
BLOCKS = 8192
ORDERS = 128
FREQS = 4096
DEGREES = 2048
N_LAT = 4
N_LON = 32


def draw_block_counts(key, part):
    key = jax.random.fold_in(key, 7)
    first_key, second_key = jax.random.split(key)
    devices = BLOCKS // BLK_DEV
    used_blocks = jax.random.randint(first_key, (devices, 1), 1, BLK_DEV + 1)
    position = jnp.arange(BLK_DEV, dtype=jnp.int32)[None, :]
    filled = jax.random.randint(second_key, (devices, BLK_DEV), PTS // 2, PTS + 1)
    counts = jnp.where(position < used_blocks, filled, 0)
    counts = jnp.where(position == 0, PTS, counts)
    return counts.reshape(BLOCKS).astype(jnp.int32)


def place_ends(entries, key, smallest, high):
    dims = entries.shape
    spot = [jax.random.randint(jax.random.fold_in(key, axis), (), 0, dims[axis]) for axis in range(len(dims))]
    entries = entries.at[tuple(spot)].set(smallest)
    longest = dims.index(max(dims))
    spot[longest] = (spot[longest] + 1) % dims[longest]
    return entries.at[tuple(spot)].set(high)


def block_scale(own_key, dims, pieces, smallest, high):
    def one(dim, shards_of):
        draws = jax.random.uniform(jax.random.fold_in(jax.random.fold_in(own_key, 6), dim), (shards_of,), jnp.float32, smallest / len(pieces), high / len(pieces))
        return jnp.repeat(jnp.exp(draws), dims[dim] // shards_of).reshape((-1,) + (1,) * (len(dims) - dim - 1))

    gain = one(*pieces[0])
    for cut in pieces[1:]:
        gain = gain * one(*cut)
    return gain


def gaussian(rng, shape, spread, reach, pieces=(), kind=jnp.bfloat16):
    gain = block_scale(rng, shape, pieces, -0.22, 0.18) if pieces else 1.0
    result = jax.random.normal(rng, shape, jnp.float32) * spread * gain
    return jnp.minimum(jnp.maximum(result, -reach), reach).astype(kind)


def setup_inputs(seed: int = 0) -> dict:
    key_of = jax.random.split(jax.random.key(seed), 8)
    point_values = gaussian(key_of[0], (2, BLOCKS, PTS), 1.0, 6.0, ((1, 128),), jnp.float32)
    theta_weights = gaussian(key_of[1], (BLOCKS, WIN_ROWS, PTS), 0.3, 1.796875, ((0, 128),))
    phi_weights = gaussian(key_of[2], (BLOCKS, WIN_COLS, PTS), 0.3, 1.796875, ((0, 128),))
    block_counts = draw_block_counts(jax.random.fold_in(key_of[7], 71), 0)
    theta_offsets = place_ends(jax.random.randint(key_of[4], (BLOCKS,), 0, ROWS_DEV + 1), jax.random.fold_in(key_of[4], 1), 0, ROWS_DEV).astype(jnp.int32)
    phi_offsets = place_ends(jax.random.randint(key_of[5], (BLOCKS,), 0, COLS_DEV + 1), jax.random.fold_in(key_of[5], 1), 0, COLS_DEV).astype(jnp.int32)
    conversion = gaussian(key_of[6], (ORDERS, FREQS, DEGREES), FREQS ** -0.5, 0.09375, ((0, 128),))
    return dict(point_values=point_values, theta_weights=theta_weights, phi_weights=phi_weights, block_counts=block_counts, theta_offsets=theta_offsets, phi_offsets=phi_offsets, conversion=conversion)


def turn_table(indices, frequencies, period):
    phase = jnp.mod(indices[:, None] * frequencies[None, :], period).astype(jnp.float32) * (2.0 * math.pi / period)
    return (jnp.cos(phase), jnp.sin(phase))

def reference(point_values, theta_weights, phi_weights, block_counts, theta_offsets, phi_offsets, conversion):
    rows_dev = GRID_ROWS // N_LAT
    cols_dev = GRID_COLS // N_LON
    win_rows = theta_weights.shape[1]
    win_cols = phi_weights.shape[1]
    points = theta_weights.shape[2]
    highest = lax.Precision.HIGHEST
    extended = jnp.zeros((2, GRID_ROWS + win_rows, GRID_COLS + win_cols), jnp.float32)

    def place(carried, inputs):
        values, row_weights, col_weights, count, row_offset, col_offset, number = inputs
        device = number // BLK_DEV
        alive = (jnp.arange(points, dtype=jnp.int32) < count).astype(jnp.float32)
        weighted = (row_weights.astype(jnp.float32)[None] * (values * alive[None])[:, None, :]).astype(jnp.bfloat16)
        window = jnp.einsum('xrp,qp->xrq', weighted.astype(jnp.float32), col_weights.astype(jnp.float32), precision=highest)
        row_start = (device // N_LON * rows_dev + row_offset).astype(jnp.int32)
        col_start = (device % N_LON * cols_dev + col_offset).astype(jnp.int32)
        anchor = jnp.zeros((), jnp.int32)
        current = lax.dynamic_slice(carried, (anchor, row_start, col_start), window.shape)
        return (lax.dynamic_update_slice(carried, current + window, (anchor, row_start, col_start)), None)
    numbers = jnp.arange(BLOCKS, dtype=jnp.int32)
    extended, _ = lax.scan(place, extended, (jnp.transpose(point_values, (1, 0, 2)), theta_weights, phi_weights, block_counts, theta_offsets, phi_offsets, numbers))
    folded = extended[:, :, :GRID_COLS].at[:, :, :win_cols].add(extended[:, :, GRID_COLS:])
    grid = folded[:, :GRID_ROWS].at[:, :win_rows].add(folded[:, GRID_ROWS:])
    orders = jnp.arange(ORDERS, dtype=jnp.int32) - ORDERS // 2
    cosines, sines = turn_table(jnp.arange(GRID_COLS, dtype=jnp.int32), orders, GRID_COLS)
    unitary = 1.0 / math.sqrt(GRID_ROWS * GRID_COLS)
    along_real = jnp.dot(grid[0], cosines, precision=highest) + jnp.dot(grid[1], sines, precision=highest)
    along_imag = jnp.dot(grid[1], cosines, precision=highest) - jnp.dot(grid[0], sines, precision=highest)
    frequencies = jnp.arange(FREQS, dtype=jnp.int32) - GRID_ROWS // 2
    row_cos, row_sin = turn_table(jnp.arange(GRID_ROWS, dtype=jnp.int32), frequencies, GRID_ROWS)
    spec_real = jnp.dot(along_real.T, row_cos, precision=highest) + jnp.dot(along_imag.T, row_sin, precision=highest)
    spec_imag = jnp.dot(along_imag.T, row_cos, precision=highest) - jnp.dot(along_real.T, row_sin, precision=highest)
    spectrum = (jnp.stack([spec_real, spec_imag], axis=1) * unitary).astype(jnp.bfloat16)

    def convert(pair):
        return jnp.dot(pair[0], pair[1], preferred_element_type=jnp.float32)
    return lax.map(convert, (spectrum, conversion))
```

```python
import functools
import math

import jax
import jax.numpy as jnp
import numpy as np
from jax import lax
from jax.experimental import pallas as pl
from jax.experimental.pallas import tpu as pltpu
from jax.sharding import PartitionSpec as P

GRID_ROWS = 4096
GRID_COLS = 8192
ORDERS = 128
BLOCKS = 64
WIN_ROWS = 32
WIN_COLS = 128
PTS = 256
ROWS_DEV = 1024
COLS_DEV = 256
EXT_ROWS = ROWS_DEV + WIN_ROWS
EXT_COLS = COLS_DEV + WIN_COLS
DEGREES = 2048
LANES = 128
T0 = 16
T1 = ROWS_DEV // T0
NX, NY, NZC = 4, 4, 8
CHUNK = 8
NCHUNK = BLOCKS // CHUNK
G_ROWS = T0 * LANES + LANES
MESH = pl.DeviceIdType.MESH
MIB = 1 << 20
BF16 = jnp.bfloat16
F32 = jnp.float32


def split_np(table):
    hi = table.astype(jnp.bfloat16)
    lo = (table - hi.astype(np.float64)).astype(jnp.bfloat16)
    return hi, lo


@functools.cache
def tables():
    place = np.arange(ORDERS)
    gx, gy, zc = place // 32, place // 8 % 4, place % 8
    order = zc * 16 + gy * 4 + gx - ORDERS // 2
    phase = (order[:, None] * np.arange(EXT_COLS)[None, :]) % GRID_COLS * (2 * np.pi / GRID_COLS)
    base = np.concatenate([np.cos(phase), np.sin(phase)]).astype(np.float32)
    turn = (order[:, None] * np.arange(32)[None, :]) % 32 * (2 * np.pi / 32)
    rot = np.zeros((ORDERS, LANES), np.float32)
    rot[:, :32] = np.cos(turn)
    rot[:, 32:64] = np.sin(turn)

    def rows_of(t1):
        angle = (t1[:, None] * np.arange(256)[None, :]) % 256 * (2 * np.pi / 256)
        return np.cos(angle), np.sin(angle)

    lane = np.arange(512)
    cos, sin = rows_of((lane // 128 * 64 + lane % 64) % 256)
    real = (lane % 128 < 64)[:, None]
    main = np.where(real, np.concatenate([cos, -sin], 1), np.concatenate([sin, cos], 1))
    cos, sin = rows_of(((lane // 128 + 1) * 64 + lane % 64 // 16) % 256)
    margin = np.where(real, np.concatenate([cos, -sin], 1), np.concatenate([sin, cos], 1))
    margin = margin * (lane % 64 < 32)[:, None]
    w_hi, w_lo = split_np(np.concatenate([main, margin]))

    unitary = 1.0 / math.sqrt(GRID_ROWS * GRID_COLS)
    angle = np.arange(16)[:, None] * np.arange(256)[None, :] * (2 * np.pi / 4096)
    twiddle = (np.concatenate([np.cos(angle), np.sin(angle)]) * unitary).astype(np.float32)

    angle = np.arange(16)[:, None] * np.arange(16)[None, :] % 16 * (2 * np.pi / 16)
    cos, sin = np.cos(angle), np.sin(angle)
    f_hi, f_lo = split_np(np.block([[cos, sin], [-sin, cos]]))
    last = np.concatenate([f_hi, f_lo, f_hi, np.zeros_like(f_hi)], 1)
    return base, rot, np.stack([w_hi, w_lo]), twiddle, last


def nt_dot(a, b):
    return lax.dot_general(a, b, (((1,), (1,)), ((), ())), preferred_element_type=F32)


def spread_kernel(counts, theta_offs, phi_offs, values, theta_hbm, phi_hbm, out, theta, phi, win, ext, sems):
    def fetch(c):
        part = pl.ds(c * CHUNK, CHUNK)
        return (
            pltpu.make_async_copy(theta_hbm.at[part], theta.at[part], sems.at[0, c]),
            pltpu.make_async_copy(phi_hbm.at[part], phi.at[part], sems.at[1, c]),
        )

    for c in range(NCHUNK):
        for copy in fetch(c):
            copy.start()

    def clear(i, carry):
        for k in range(4):
            for x in range(2):
                ext[k, x, pl.ds(pl.multiple_of(i * 96, 8), 96), :] = jnp.zeros((96, LANES), F32)
        return carry

    lax.fori_loop(0, EXT_ROWS // 96, clear, 0)
    point = lax.broadcasted_iota(jnp.int32, (1, PTS), 1)
    lane = lax.broadcasted_iota(jnp.int32, (WIN_ROWS, LANES), 1)

    def step(c, carry):
        for copy in fetch(c):
            copy.wait()
        for n in range(CHUNK):
            b = c * CHUNK + n
            live = point < counts[b]
            rows = theta[b].astype(F32)
            parts = []
            for x in range(2):
                own = jnp.where(live, values[x, pl.ds(b, 1), :], 0.0)
                parts.append((rows * own).astype(BF16))
            win[n] = nt_dot(jnp.concatenate(parts, 0), phi[b])
        for n in range(CHUNK):
            b = c * CHUNK + n
            row = theta_offs[b]
            col = phi_offs[b]
            tile = col // LANES
            shift = col % LANES
            near = lane >= shift
            for x in range(2):
                moved = pltpu.roll(win[n, x * WIN_ROWS : (x + 1) * WIN_ROWS, :], shift, 1)
                here = pl.ds(row, WIN_ROWS)
                ext[tile, x, here, :] += jnp.where(near, moved, 0.0)
                ext[tile + 1, x, here, :] += jnp.where(near, 0.0, moved)
        return carry

    lax.fori_loop(0, NCHUNK, step, 0)

    for k in range(3):
        cols = slice(k * LANES, (k + 1) * LANES)
        for x in range(2):
            for t0 in range(T0):
                at = t0 * LANES + x * T1
                out[at : at + T1, cols] = ext[k, x, pl.ds(t0, T1, stride=T0), :].astype(BF16)
            at = T0 * LANES + x * T1
            out[at : at + 32, cols] = ext[k, x, ROWS_DEV:EXT_ROWS, :].astype(BF16)
            out[at + 32 : at + 64, cols] = jnp.zeros((32, LANES), BF16)


def spread(point_values, theta_weights, phi_weights, block_counts, theta_offsets, phi_offsets):
    smem = pl.BlockSpec(memory_space=pltpu.SMEM)
    vmem = pl.BlockSpec(memory_space=pltpu.VMEM)
    hbm = pl.BlockSpec(memory_space=pl.ANY)
    return pl.pallas_call(
        spread_kernel,
        out_shape=jax.ShapeDtypeStruct((G_ROWS, EXT_COLS), BF16),
        in_specs=[smem, smem, smem, vmem, hbm, hbm],
        out_specs=vmem,
        scratch_shapes=[
            pltpu.VMEM((BLOCKS, WIN_ROWS, PTS), BF16),
            pltpu.VMEM((BLOCKS, WIN_COLS, PTS), BF16),
            pltpu.VMEM((CHUNK, 2 * WIN_ROWS, WIN_COLS), F32),
            pltpu.VMEM((4, 2, EXT_ROWS, LANES), F32),
            pltpu.SemaphoreType.DMA((2, NCHUNK)),
        ],
        compiler_params=pltpu.CompilerParams(vmem_limit_bytes=32 * MIB),
        name="spread",
    )(block_counts, theta_offsets, phi_offsets, point_values, theta_weights, phi_weights)


def split(value):
    hi = value.astype(BF16)
    return hi, (value - hi.astype(F32)).astype(BF16)


def finish_kernel(
    base, rot, twiddle, last, g_hbm, w_hbm, conv_hbm, out,
    g, w, conv, d, a, b, got_a, got_b, sum_a, sum_b, got_a2, got_b2, q, qz, r, spec,
    load_sem, conv_sem, send_a, recv_a, send_b, recv_b, send_a2, recv_a2, send_b2, recv_b2, send_z, recv_z,
):
    lat = lax.axis_index("lat")
    lon = lax.axis_index("lon")
    z_lo = lon // 16
    my = lon // 4 % 4
    mx = lon % 4
    zc = lat * 2 + z_lo

    def x_peer(by):
        to = lax.rem(mx + by, NX)
        return to, (lat, z_lo * 16 + my * 4 + to)

    def y_peer(by):
        to = lax.rem(my + by, NY)
        return to, (lat, z_lo * 16 + to * 4 + mx)

    def z_peer(by):
        to = lax.rem(zc + by, NZC)
        return to, (to // 2, to % 2 * 16 + my * 4 + mx)

    barrier = pltpu.get_barrier_semaphore()
    for peer, count in ((x_peer, NX), (y_peer, NY), (z_peer, NZC)):
        for by in range(1, count):
            pl.semaphore_signal(barrier, inc=1, device_id=peer(by)[1], device_id_type=MESH)

    half = T0 * LANES // 2
    loads = [
        pltpu.make_async_copy(g_hbm.at[pl.ds(0, half)], g.at[pl.ds(0, half)], load_sem.at[0]),
        pltpu.make_async_copy(g_hbm.at[pl.ds(half, G_ROWS - half)], g.at[pl.ds(half, G_ROWS - half)], load_sem.at[1]),
        pltpu.make_async_copy(w_hbm, w, load_sem.at[2]),
    ]
    for copy in loads:
        copy.start()
    conv_loads = [
        pltpu.make_async_copy(conv_hbm.at[0, pl.ds(k * 1024, 1024)], conv.at[pl.ds(k * 1024, 1024)], conv_sem.at[k])
        for k in range(4)
    ]
    for copy in conv_loads:
        copy.start()

    lane = lax.broadcasted_iota(jnp.int32, (ORDERS, LANES), 1)
    turn = rot[...]
    turn_cos = jnp.sum(jnp.where(lane == lon, turn, 0.0), axis=1, keepdims=True)
    turn_sin = jnp.sum(jnp.where(lane == lon + 32, turn, 0.0), axis=1, keepdims=True)
    cos, sin = base[:ORDERS, :], base[ORDERS:, :]
    here_cos = cos * turn_cos - sin * turn_sin
    here_sin = sin * turn_cos + cos * turn_sin
    cos_hi, cos_lo = split(here_cos)
    sin_hi, sin_lo = split(here_sin)
    d[0:128, :] = cos_hi
    d[128:256, :] = sin_hi
    d[256:384, :] = cos_lo
    d[384:512, :] = sin_lo

    first = lax.broadcasted_iota(jnp.int32, (ORDERS, LANES), 1) < 64

    def along(product, at):
        cut = slice(at * LANES, (at + 1) * LANES)
        by_cos = product[0:128, cut] + product[256:384, cut]
        by_sin = pltpu.roll(product[128:256, cut] + product[384:512, cut], 64, 1)
        return (by_cos + jnp.where(first, by_sin, -by_sin)).reshape(NX, NY, NZC, LANES)

    loads[0].wait()
    for pair in range(4):
        product = nt_dot(d[...], g[pair * 256 : pair * 256 + 256, :])
        for at in range(2):
            a[:, :, pair * 2 + at, :, :] = along(product, at)
    pl.semaphore_wait(barrier, (NX - 1) + (NY - 1) + (NZC - 1))

    def exchange(source, dest, peer, send, recv):
        copies = []
        for by in range(1, 4):
            to, device = peer(by)
            copies.append(pltpu.make_async_remote_copy(
                src_ref=source(to), dst_ref=dest.at[by - 1], send_sem=send.at[by - 1], recv_sem=recv.at[by - 1],
                device_id=device, device_id_type=MESH,
            ))
        for copy in copies:
            copy.start()
        return copies

    copies_a = exchange(lambda to: a.at[to], got_a, x_peer, send_a, recv_a)
    loads[1].wait()
    for pair in range(4):
        product = nt_dot(d[...], g[half + pair * 256 : half + pair * 256 + 256, :])
        for at in range(2):
            b[:, :, pair * 2 + at, :, :] = along(product, at)
    b[:, :, 8, :, :] = along(nt_dot(d[...], g[T0 * LANES : G_ROWS, :]), 0)
    copies_b = exchange(lambda to: b.at[:, to], got_b, y_peer, send_b, recv_b)

    for copy in copies_a:
        copy.wait_recv()
    sum_a[...] = (a[mx] + got_a[0]) + (got_a[1] + got_a[2])
    copies_a2 = exchange(lambda to: sum_a.at[to], got_a2, y_peer, send_a2, recv_a2)
    for copy in copies_b:
        copy.wait_recv()
    sum_b[...] = (b[:, my] + got_b[0]) + (got_b[1] + got_b[2])
    copies_b2 = exchange(lambda to: sum_b.at[to], got_b2, x_peer, send_b2, recv_b2)

    q[17 * 8 :, :] = jnp.zeros((7 * 8, LANES), F32)
    for copy in copies_a2:
        copy.wait_recv()
    q[0:64, :] = ((sum_a[my] + got_a2[0]) + (got_a2[1] + got_a2[2])).reshape(64, LANES)
    for copy in copies_b2:
        copy.wait_recv()
    q[64:136, :] = ((sum_b[mx] + got_b2[0]) + (got_b2[1] + got_b2[2])).reshape(72, LANES)
    for z in range(NZC):
        qz[z] = q[pl.ds(z, 24, stride=8), :]

    copies_z = []
    for by in range(1, NZC):
        to, device = z_peer(by)
        copies_z.append(pltpu.make_async_remote_copy(
            src_ref=qz.at[to], dst_ref=r.at[zc], send_sem=send_z.at[by - 1], recv_sem=recv_z.at[by - 1],
            device_id=device, device_id_type=MESH,
        ))
    for copy in copies_z:
        copy.start()
    r[zc] = qz[zc]
    loads[2].wait()
    for copy in copies_z:
        copy.wait_recv()

    tiles = [r[2 * i] + r[2 * i + 1] for i in range(4)]
    row = lax.broadcasted_iota(jnp.int32, (T0, LANES), 0)
    col = lax.broadcasted_iota(jnp.int32, (T0, LANES), 1)
    keep = (col % T0 == row) & (col % 64 < 32)
    margins = [jnp.where(keep, jnp.broadcast_to(tile[16:17, :], (T0, LANES)), 0.0) for tile in tiles]
    sums = jnp.concatenate([tile[0:16, :] for tile in tiles] + margins, 1)
    hi, lo = split(sums)
    both = jnp.dot(jnp.concatenate([hi, lo], 0), w[0], preferred_element_type=F32)
    inner = both[0:16] + both[16:32] + jnp.dot(hi, w[1], preferred_element_type=F32)
    real, imag = inner[:, :256], inner[:, 256:]
    cos, sin = twiddle[0:16, :], twiddle[16:32, :]
    turned = jnp.concatenate([real * cos + imag * sin, imag * cos - real * sin], 0)
    hi, lo = split(turned)
    stacked = jnp.concatenate([hi, hi, lo, jnp.zeros_like(hi)], 0)
    spectrum = jnp.dot(last[...], stacked, preferred_element_type=F32)
    hi, lo = split(spectrum)
    for side in range(2):
        cut = slice(side * LANES, (side + 1) * LANES)
        spec[side, 0:32, :] = hi[:, cut].astype(F32)
        spec[side, 32:64, :] = lo[:, cut].astype(F32)

    total = jnp.zeros((4, DEGREES), F32)
    for block in range(16):
        if block % 4 == 0:
            conv_loads[block // 4].wait()
        here = pl.ds((block + 8) % 16, 4, stride=16)
        rows = jnp.concatenate([spec[0, here, :], spec[1, here, :]], 1).astype(BF16)
        total += jnp.dot(rows, conv[block * 256 : block * 256 + 256, :], preferred_element_type=F32)
    out[0] = total[0:2] + total[2:4]

    for group in (copies_a, copies_b, copies_a2, copies_b2, copies_z):
        for copy in group:
            copy.wait_send()


def finish(g, conversion):
    base, rot, w, twiddle, last = (jnp.asarray(table) for table in tables())
    vmem = pl.BlockSpec(memory_space=pltpu.VMEM)
    hbm = pl.BlockSpec(memory_space=pl.ANY)
    dma = pltpu.SemaphoreType.DMA
    return pl.pallas_call(
        finish_kernel,
        out_shape=jax.ShapeDtypeStruct((1, 2, DEGREES), F32),
        in_specs=[vmem, vmem, vmem, vmem, hbm, hbm, hbm],
        out_specs=vmem,
        scratch_shapes=[
            pltpu.VMEM((G_ROWS, EXT_COLS), BF16),
            pltpu.VMEM((2, 1024, 512), BF16),
            pltpu.VMEM((GRID_ROWS, DEGREES), BF16),
            pltpu.VMEM((512, EXT_COLS), BF16),
            pltpu.VMEM((NX, NY, 8, NZC, LANES), F32),
            pltpu.VMEM((NX, NY, 9, NZC, LANES), F32),
            pltpu.VMEM((3, NY, 8, NZC, LANES), F32),
            pltpu.VMEM((3, NX, 9, NZC, LANES), F32),
            pltpu.VMEM((NY, 8, NZC, LANES), F32),
            pltpu.VMEM((NX, 9, NZC, LANES), F32),
            pltpu.VMEM((3, 8, NZC, LANES), F32),
            pltpu.VMEM((3, 9, NZC, LANES), F32),
            pltpu.VMEM((24 * 8, LANES), F32),
            pltpu.VMEM((NZC, 24, LANES), F32),
            pltpu.VMEM((NZC, 24, LANES), F32),
            pltpu.VMEM((2, 64, LANES), F32),
            dma((3,)), dma((4,)),
            dma((3,)), dma((3,)), dma((3,)), dma((3,)),
            dma((3,)), dma((3,)), dma((3,)), dma((3,)),
            dma((7,)), dma((7,)),
        ],
        compiler_params=pltpu.CompilerParams(
            collective_id=0, has_side_effects=True, vmem_limit_bytes=48 * MIB
        ),
        name="finish",
    )(base, rot, twiddle, last, g, w, conversion)


def shards(
    point_values, theta_weights, phi_weights, block_counts, theta_offsets, phi_offsets, conversion
):
    g = spread(point_values, theta_weights, phi_weights, block_counts, theta_offsets, phi_offsets)
    return finish(g, conversion)


def solution(mesh):
    placed = (
        P(None, ("lat", "lon"), None),
        P(("lat", "lon"), None, None),
        P(("lat", "lon"), None, None),
        P(("lat", "lon")),
        P(("lat", "lon")),
        P(("lat", "lon")),
        P(("lat", "lon"), None, None),
    )
    return jax.shard_map(
        shards, mesh=mesh, in_specs=placed, out_specs=P(("lat", "lon"), None, None), check_vma=False
    )
```

```python
import functools
import math

import jax
import jax.numpy as jnp
import numpy as np
from jax import lax
from jax.experimental import pallas as pl
from jax.experimental.pallas import tpu as pltpu
from jax.sharding import PartitionSpec as P

GRID_ROWS = 4096
GRID_COLS = 8192
ORDERS = 128
BLOCKS = 64
WIN_ROWS = 32
WIN_COLS = 128
PTS = 256
ROWS_DEV = 1024
COLS_DEV = 256
EXT_ROWS = ROWS_DEV + WIN_ROWS
EXT_COLS = COLS_DEV + WIN_COLS
DEGREES = 2048
LANES = 128
T0 = 64
T1 = ROWS_DEV // T0
NX, NY, NZC = 4, 4, 8
CHUNK = 8
NCHUNK = BLOCKS // CHUNK
G_ROWS = T1 * LANES + LANES
MESH = pl.DeviceIdType.MESH
MIB = 1 << 20
BF16 = jnp.bfloat16
F32 = jnp.float32


def split_np(table):
    hi = table.astype(jnp.bfloat16)
    lo = (table - hi.astype(np.float64)).astype(jnp.bfloat16)
    return hi, lo


@functools.cache
def tables():
    place = np.arange(ORDERS)
    gx, gy, zc = place // 32, place // 8 % 4, place % 8
    order = zc * 16 + gy * 4 + gx - ORDERS // 2
    phase = (order[:, None] * np.arange(EXT_COLS)[None, :]) % GRID_COLS * (2 * np.pi / GRID_COLS)
    base = np.concatenate([np.cos(phase), np.sin(phase)]).astype(np.float32)
    turn = (order[:, None] * np.arange(32)[None, :]) % 32 * (2 * np.pi / 32)
    rot = np.zeros((ORDERS, LANES), np.float32)
    rot[:, :32] = np.cos(turn)
    rot[:, 32:64] = np.sin(turn)

    index = np.arange(64)
    angle = index[:, None] * index[None, :] % 64 * (2 * np.pi / 64)
    cos, sin = np.cos(angle), np.sin(angle)
    hi, lo = split_np(np.concatenate([cos, sin]))
    first = np.concatenate([hi, lo, hi, np.zeros_like(hi)], 1)
    unitary = 1.0 / math.sqrt(GRID_ROWS * GRID_COLS)
    angle = index[:, None] * index[None, :] * (2 * np.pi / 4096)
    twiddle = np.stack([
        np.concatenate([np.cos(angle), np.cos(angle)], 1), np.concatenate([np.sin(angle), -np.sin(angle)], 1)
    ])
    twiddle = (twiddle * unitary).astype(np.float32)
    second = np.block([[cos, sin], [-sin, cos]]).reshape(2, 16, 4, 128).transpose(2, 0, 1, 3).reshape(128, 128)
    hi, lo = split_np(second)
    second = np.concatenate([hi, lo, hi], 1)
    return base, rot, first, twiddle, second


def nt_dot(a, b):
    return lax.dot_general(a, b, (((1,), (1,)), ((), ())), preferred_element_type=F32)


def spread_kernel(
    counts_hbm, theta_offs_hbm, phi_offs_hbm, base_hbm, rot_hbm, values_hbm, theta_hbm, phi_hbm, out, d,
    counts, theta_offs, phi_offs, base, rot, values, theta, phi, win_a, win_b, ext, sems, small_sems,
):
    small = [
        pltpu.make_async_copy(source, dest, small_sems.at[k])
        for k, (source, dest) in enumerate((
            (rot_hbm, rot), (base_hbm, base), (counts_hbm, counts), (theta_offs_hbm, theta_offs),
            (phi_offs_hbm, phi_offs), (values_hbm, values),
        ))
    ]
    for copy in small:
        copy.start()

    def fetch(c):
        part = pl.ds(c * CHUNK, CHUNK)
        return (
            pltpu.make_async_copy(theta_hbm.at[part], theta.at[part], sems.at[0, c]),
            pltpu.make_async_copy(phi_hbm.at[part], phi.at[part], sems.at[1, c]),
        )

    for c in range(NCHUNK):
        for copy in fetch(c):
            copy.start()

    def clear(i, carry):
        for k in range(4):
            for x in range(2):
                ext[k, x, pl.ds(pl.multiple_of(i * 96, 8), 96), :] = jnp.zeros((96, LANES), F32)
        return carry

    lax.fori_loop(0, EXT_ROWS // 96, clear, 0)

    for copy in small[:2]:
        copy.wait()
    lon = lax.axis_index("lon")
    place_of = lax.broadcasted_iota(jnp.int32, (ORDERS, LANES), 1)
    turn = rot[...]
    turn_cos = jnp.sum(jnp.where(place_of == lon, turn, 0.0), axis=1, keepdims=True)
    turn_sin = jnp.sum(jnp.where(place_of == lon + 32, turn, 0.0), axis=1, keepdims=True)
    cos, sin = base[:ORDERS, :], base[ORDERS:, :]
    cos_hi, cos_lo = split(cos * turn_cos - sin * turn_sin)
    sin_hi, sin_lo = split(sin * turn_cos + cos * turn_sin)
    d[0:128, :] = cos_hi
    d[128:256, :] = sin_hi
    d[256:384, :] = cos_lo
    d[384:512, :] = sin_lo

    point = lax.broadcasted_iota(jnp.int32, (1, PTS), 1)
    lane = lax.broadcasted_iota(jnp.int32, (WIN_ROWS, LANES), 1)

    def windows(c, win):
        for copy in fetch(c):
            copy.wait()
        for n in range(CHUNK):
            b = c * CHUNK + n
            live = point < counts[b]
            rows = theta[b].astype(F32)
            parts = []
            for x in range(2):
                own = jnp.where(live, values[x, pl.ds(b, 1), :], 0.0)
                parts.append((rows * own).astype(BF16))
            win[n] = nt_dot(jnp.concatenate(parts, 0), phi[b])

    def place(c, win):
        for n in range(CHUNK):
            b = c * CHUNK + n
            row = theta_offs[b]
            col = phi_offs[b]
            tile = col // LANES
            shift = col % LANES
            near = lane >= shift
            here = pl.ds(row, WIN_ROWS)
            for x in range(2):
                moved = pltpu.roll(win[n, x * WIN_ROWS : (x + 1) * WIN_ROWS, :], shift, 1)
                ext[tile, x, here, :] += jnp.where(near, moved, 0.0)
                ext[tile + 1, x, here, :] += jnp.where(near, 0.0, moved)

    for copy in small[2:]:
        copy.wait()
    windows(0, win_a)

    def step(i, carry):
        windows(2 * i + 1, win_b)
        place(2 * i, win_a)
        windows(2 * i + 2, win_a)
        place(2 * i + 1, win_b)
        return carry

    lax.fori_loop(0, NCHUNK // 2 - 1, step, 0)
    windows(NCHUNK - 1, win_b)
    place(NCHUNK - 2, win_a)
    place(NCHUNK - 1, win_b)

    for k in range(3):
        cols = slice(k * LANES, (k + 1) * LANES)
        for x in range(2):
            for t1 in range(T1):
                at = t1 * LANES + x * T0
                out[at : at + T0, cols] = ext[k, x, t1 * T0 : (t1 + 1) * T0, :].astype(BF16)
            at = T1 * LANES + x * T0
            out[at : at + 32, cols] = ext[k, x, ROWS_DEV:EXT_ROWS, :].astype(BF16)
            out[at + 32 : at + 64, cols] = jnp.zeros((32, LANES), BF16)


def spread(point_values, theta_weights, phi_weights, block_counts, theta_offsets, phi_offsets):
    base, rot = (jnp.asarray(table) for table in tables()[:2])
    vmem = pl.BlockSpec(memory_space=pltpu.VMEM)
    operands = [block_counts, theta_offsets, phi_offsets, base, rot, point_values, theta_weights, phi_weights]
    return pl.pallas_call(
        spread_kernel,
        out_shape=(
            jax.ShapeDtypeStruct((G_ROWS, EXT_COLS), BF16),
            jax.ShapeDtypeStruct((4 * ORDERS, EXT_COLS), BF16),
        ),
        in_specs=[pl.BlockSpec(memory_space=pltpu.HBM)] * len(operands),
        out_specs=(vmem, vmem),
        scratch_shapes=[
            pltpu.SMEM((BLOCKS,), jnp.int32),
            pltpu.SMEM((BLOCKS,), jnp.int32),
            pltpu.SMEM((BLOCKS,), jnp.int32),
            pltpu.VMEM((2 * ORDERS, EXT_COLS), F32),
            pltpu.VMEM((ORDERS, LANES), F32),
            pltpu.VMEM((2, BLOCKS, PTS), F32),
            pltpu.VMEM((BLOCKS, WIN_ROWS, PTS), BF16),
            pltpu.VMEM((BLOCKS, WIN_COLS, PTS), BF16),
            pltpu.VMEM((CHUNK, 2 * WIN_ROWS, WIN_COLS), F32),
            pltpu.VMEM((CHUNK, 2 * WIN_ROWS, WIN_COLS), F32),
            pltpu.VMEM((4, 2, EXT_ROWS, LANES), F32),
            pltpu.SemaphoreType.DMA((2, NCHUNK)),
            pltpu.SemaphoreType.DMA((6,)),
        ],
        compiler_params=pltpu.CompilerParams(vmem_limit_bytes=32 * MIB),
        name="spread",
    )(*(pltpu.with_memory_space_constraint(operand, pltpu.HBM) for operand in operands))


def split(value):
    hi = value.astype(BF16)
    return hi, (value - hi.astype(F32)).astype(BF16)


def finish_kernel(
    g, d, first, twiddle, second, conv_hbm, out,
    conv, a, b, got_a, got_b, sum_a, sum_b, got_a2, got_b2, q, qz, r, spec,
    conv_sem, send_a, recv_a, send_b, recv_b, send_a2, recv_a2, send_b2, recv_b2, send_z, recv_z,
):
    lat = lax.axis_index("lat")
    lon = lax.axis_index("lon")
    z_lo = lon // 16
    my = lon // 4 % 4
    mx = lon % 4
    zc = lat * 2 + z_lo

    def x_peer(by):
        to = lax.rem(mx + by, NX)
        return to, (lat, z_lo * 16 + my * 4 + to)

    def y_peer(by):
        to = lax.rem(my + by, NY)
        return to, (lat, z_lo * 16 + to * 4 + mx)

    def z_peer(by):
        to = lax.rem(zc + by, NZC)
        return to, (to // 2, to % 2 * 16 + my * 4 + mx)

    barrier = pltpu.get_barrier_semaphore()
    for peer, count in ((x_peer, NX), (y_peer, NY), (z_peer, NZC)):
        for by in range(1, count):
            pl.semaphore_signal(barrier, inc=1, device_id=peer(by)[1], device_id_type=MESH)

    half = T1 * LANES // 2
    conv_loads = [
        pltpu.make_async_copy(conv_hbm.at[0, pl.ds(k * 1024, 1024)], conv.at[pl.ds(k * 1024, 1024)], conv_sem.at[k])
        for k in range(4)
    ]
    for copy in conv_loads:
        copy.start()

    early = lax.broadcasted_iota(jnp.int32, (ORDERS, LANES), 1) < 64

    def along(product, at):
        cut = slice(at * LANES, (at + 1) * LANES)
        by_cos = product[0:128, cut] + product[256:384, cut]
        by_sin = pltpu.roll(product[128:256, cut] + product[384:512, cut], 64, 1)
        return (by_cos + jnp.where(early, by_sin, -by_sin)).reshape(NX, NY, NZC, LANES)

    for pair in range(4):
        product = nt_dot(d[...], g[pair * 256 : pair * 256 + 256, :])
        for at in range(2):
            a[:, :, pair * 2 + at, :, :] = along(product, at)
    pl.semaphore_wait(barrier, (NX - 1) + (NY - 1) + (NZC - 1))

    def exchange(source, dest, peer, send, recv):
        copies = []
        for by in range(1, 4):
            to, device = peer(by)
            copies.append(pltpu.make_async_remote_copy(
                src_ref=source(to), dst_ref=dest.at[by - 1], send_sem=send.at[by - 1], recv_sem=recv.at[by - 1],
                device_id=device, device_id_type=MESH,
            ))
        for copy in copies:
            copy.start()
        return copies

    copies_a = exchange(lambda to: a.at[to], got_a, x_peer, send_a, recv_a)
    for pair in range(4):
        product = nt_dot(d[...], g[half + pair * 256 : half + pair * 256 + 256, :])
        for at in range(2):
            b[:, :, pair * 2 + at, :, :] = along(product, at)
    b[:, :, 8, :, :] = along(nt_dot(d[...], g[T1 * LANES : G_ROWS, :]), 0)
    copies_b = exchange(lambda to: b.at[:, to], got_b, y_peer, send_b, recv_b)

    for copy in copies_a:
        copy.wait_recv()
    sum_a[...] = (a[mx] + got_a[0]) + (got_a[1] + got_a[2])
    copies_a2 = exchange(lambda to: sum_a.at[to], got_a2, y_peer, send_a2, recv_a2)
    for copy in copies_b:
        copy.wait_recv()
    sum_b[...] = (b[:, my] + got_b[0]) + (got_b[1] + got_b[2])
    copies_b2 = exchange(lambda to: sum_b.at[to], got_b2, x_peer, send_b2, recv_b2)

    q[17 * 8 :, :] = jnp.zeros((7 * 8, LANES), F32)
    for copy in copies_a2:
        copy.wait_recv()
    q[0:64, :] = ((sum_a[my] + got_a2[0]) + (got_a2[1] + got_a2[2])).reshape(64, LANES)
    for copy in copies_b2:
        copy.wait_recv()
    q[64:136, :] = ((sum_b[mx] + got_b2[0]) + (got_b2[1] + got_b2[2])).reshape(72, LANES)
    for z in range(NZC):
        qz[z] = q[pl.ds(z, 24, stride=8), :]

    copies_z = []
    for by in range(1, NZC):
        to, device = z_peer(by)
        copies_z.append(pltpu.make_async_remote_copy(
            src_ref=qz.at[to], dst_ref=r.at[zc], send_sem=send_z.at[by - 1], recv_sem=recv_z.at[by - 1],
            device_id=device, device_id_type=MESH,
        ))
    for copy in copies_z:
        copy.start()
    r[zc] = qz[zc]
    for copy in copies_z:
        copy.wait_recv()

    tiles = [r[2 * i] + r[2 * i + 1] for i in range(4)]
    top = lax.broadcasted_iota(jnp.int32, (T1, LANES), 0) == 0
    rows = [
        tile[0:T1, :] + jnp.where(top, jnp.broadcast_to(above[T1 : T1 + 1, :], (T1, LANES)), 0.0)
        for tile, above in zip(tiles, tiles[3:] + tiles[:3])
    ]
    hi, lo = split(jnp.concatenate(rows, 0))
    both = jnp.dot(first[...], jnp.concatenate([hi, hi, lo, jnp.zeros_like(hi)], 0), preferred_element_type=F32)
    by_sin = pltpu.roll(both[64:128], 64, 1)
    inner = both[0:64] + jnp.where(early[0:64], by_sin, -by_sin)
    turned = inner * twiddle[0] + pltpu.roll(inner, 64, 1) * twiddle[1]
    hi, lo = split(turned)
    parts = nt_dot(second[...], jnp.concatenate([hi, hi, lo], 1))
    hi, lo = split(jnp.concatenate([parts[32 * j : 32 * j + 32] for j in range(4)], 1))
    for side in range(2):
        cut = slice(side * LANES, (side + 1) * LANES)
        spec[side, 0:32, :] = hi[:, cut].astype(F32)
        spec[side, 32:64, :] = lo[:, cut].astype(F32)

    total = jnp.zeros((4, DEGREES), F32)
    for block in range(16):
        if block % 4 == 0:
            conv_loads[block // 4].wait()
        here = pl.ds((block + 8) % 16, 4, stride=16)
        rows = jnp.concatenate([spec[0, here, :], spec[1, here, :]], 1).astype(BF16)
        total += jnp.dot(rows, conv[block * 256 : block * 256 + 256, :], preferred_element_type=F32)
    out[0] = total[0:2] + total[2:4]

    for group in (copies_a, copies_b, copies_a2, copies_b2, copies_z):
        for copy in group:
            copy.wait_send()


def finish(g, d, conversion):
    first, twiddle, second = (jnp.asarray(table) for table in tables()[2:])
    vmem = pl.BlockSpec(memory_space=pltpu.VMEM)
    hbm = pl.BlockSpec(memory_space=pl.ANY)
    dma = pltpu.SemaphoreType.DMA
    return pl.pallas_call(
        finish_kernel,
        out_shape=jax.ShapeDtypeStruct((1, 2, DEGREES), F32),
        in_specs=[vmem, vmem, vmem, vmem, vmem, hbm],
        out_specs=vmem,
        scratch_shapes=[
            pltpu.VMEM((GRID_ROWS, DEGREES), BF16),
            pltpu.VMEM((NX, NY, 8, NZC, LANES), F32),
            pltpu.VMEM((NX, NY, 9, NZC, LANES), F32),
            pltpu.VMEM((3, NY, 8, NZC, LANES), F32),
            pltpu.VMEM((3, NX, 9, NZC, LANES), F32),
            pltpu.VMEM((NY, 8, NZC, LANES), F32),
            pltpu.VMEM((NX, 9, NZC, LANES), F32),
            pltpu.VMEM((3, 8, NZC, LANES), F32),
            pltpu.VMEM((3, 9, NZC, LANES), F32),
            pltpu.VMEM((24 * 8, LANES), F32),
            pltpu.VMEM((NZC, 24, LANES), F32),
            pltpu.VMEM((NZC, 24, LANES), F32),
            pltpu.VMEM((2, 64, LANES), F32),
            dma((4,)),
            dma((3,)), dma((3,)), dma((3,)), dma((3,)),
            dma((3,)), dma((3,)), dma((3,)), dma((3,)),
            dma((7,)), dma((7,)),
        ],
        compiler_params=pltpu.CompilerParams(
            collective_id=0, has_side_effects=True, vmem_limit_bytes=48 * MIB
        ),
        name="finish",
    )(g, d, first, twiddle, second, conversion)


def shards(
    point_values, theta_weights, phi_weights, block_counts, theta_offsets, phi_offsets, conversion
):
    g, d = spread(point_values, theta_weights, phi_weights, block_counts, theta_offsets, phi_offsets)
    return finish(g, d, conversion)


def solution(mesh):
    placed = (
        P(None, ("lat", "lon"), None),
        P(("lat", "lon"), None, None),
        P(("lat", "lon"), None, None),
        P(("lat", "lon")),
        P(("lat", "lon")),
        P(("lat", "lon")),
        P(("lat", "lon"), None, None),
    )
    return jax.shard_map(
        shards, mesh=mesh, in_specs=placed, out_specs=P(("lat", "lon"), None, None), check_vma=False
    )
```

```python
import functools
import math

import jax
import jax.numpy as jnp
import numpy as np
from jax import lax
from jax.experimental import pallas as pl
from jax.experimental.pallas import tpu as pltpu
from jax.sharding import PartitionSpec as P

GRID_ROWS = 4096
GRID_COLS = 8192
ORDERS = 128
BLOCKS = 64
WIN_ROWS = 32
WIN_COLS = 128
PTS = 256
ROWS_DEV = 1024
COLS_DEV = 256
EXT_ROWS = ROWS_DEV + WIN_ROWS
EXT_COLS = COLS_DEV + WIN_COLS
DEGREES = 2048
LANES = 128
T0 = 64
T1 = ROWS_DEV // T0
NX, NY, NZC = 4, 4, 8
CHUNK = 8
NCHUNK = BLOCKS // CHUNK
G_ROWS = T1 * LANES + LANES
MESH = pl.DeviceIdType.MESH
MIB = 1 << 20
BF16 = jnp.bfloat16
F32 = jnp.float32


def split_np(table):
    hi = table.astype(jnp.bfloat16)
    lo = (table - hi.astype(np.float64)).astype(jnp.bfloat16)
    return hi, lo


@functools.cache
def tables():
    place = np.arange(ORDERS)
    gx, gy, zc = place // 32, place // 8 % 4, place % 8
    order = zc * 16 + gy * 4 + gx - ORDERS // 2
    phase = (order[:, None] * np.arange(EXT_COLS)[None, :]) % GRID_COLS * (2 * np.pi / GRID_COLS)
    base = np.concatenate([np.cos(phase), np.sin(phase)]).astype(np.float32)
    turn = (order[:, None] * np.arange(32)[None, :]) % 32 * (2 * np.pi / 32)
    rot = np.zeros((ORDERS, LANES), np.float32)
    rot[:, :32] = np.cos(turn)
    rot[:, 32:64] = np.sin(turn)

    index = np.arange(64)
    angle = index[:, None] * index[None, :] % 64 * (2 * np.pi / 64)
    cos, sin = np.cos(angle), np.sin(angle)
    hi, lo = split_np(np.concatenate([cos, sin]))
    first = np.concatenate([hi, lo, hi, np.zeros_like(hi)], 1)
    unitary = 1.0 / math.sqrt(GRID_ROWS * GRID_COLS)
    angle = index[:, None] * index[None, :] * (2 * np.pi / 4096)
    twiddle = np.stack([
        np.concatenate([np.cos(angle), np.cos(angle)], 1), np.concatenate([np.sin(angle), -np.sin(angle)], 1)
    ])
    twiddle = (twiddle * unitary).astype(np.float32)
    second = np.block([[cos, sin], [-sin, cos]]).reshape(2, 16, 4, 128).transpose(2, 0, 1, 3).reshape(128, 128)
    hi, lo = split_np(second)
    second = np.concatenate([hi, lo, hi], 1)
    return base, rot, first, twiddle, second


def nt_dot(a, b):
    return lax.dot_general(a, b, (((1,), (1,)), ((), ())), preferred_element_type=F32)


def spread_kernel(
    counts_hbm, theta_offs_hbm, phi_offs_hbm, base_hbm, rot_hbm, values_hbm, theta_hbm, phi_hbm, out, d,
    counts, theta_offs, phi_offs, base, rot, values, theta, phi, win_a, win_b, ext, sems, small_sems,
):
    small = [
        pltpu.make_async_copy(source, dest, small_sems.at[k])
        for k, (source, dest) in enumerate((
            (rot_hbm, rot), (base_hbm, base), (counts_hbm, counts), (theta_offs_hbm, theta_offs),
            (phi_offs_hbm, phi_offs), (values_hbm, values),
        ))
    ]
    for copy in small:
        copy.start()

    def fetch(c):
        part = pl.ds(c * CHUNK, CHUNK)
        return (
            pltpu.make_async_copy(theta_hbm.at[part], theta.at[part], sems.at[0, c]),
            pltpu.make_async_copy(phi_hbm.at[part], phi.at[part], sems.at[1, c]),
        )

    for c in range(4):
        for copy in fetch(c):
            copy.start()

    def clear(i, carry):
        for k in range(4):
            for x in range(2):
                ext[k, x, pl.ds(pl.multiple_of(i * 96, 8), 96), :] = jnp.zeros((96, LANES), F32)
        return carry

    lax.fori_loop(0, EXT_ROWS // 96, clear, 0)

    for copy in small[:2]:
        copy.wait()
    lon = lax.axis_index("lon")
    place_of = lax.broadcasted_iota(jnp.int32, (ORDERS, LANES), 1)
    turn = rot[...]
    turn_cos = jnp.sum(jnp.where(place_of == lon, turn, 0.0), axis=1, keepdims=True)
    turn_sin = jnp.sum(jnp.where(place_of == lon + 32, turn, 0.0), axis=1, keepdims=True)
    cos, sin = base[:ORDERS, :], base[ORDERS:, :]
    cos_hi, cos_lo = split(cos * turn_cos - sin * turn_sin)
    sin_hi, sin_lo = split(sin * turn_cos + cos * turn_sin)
    d[0:128, :] = cos_hi
    d[128:256, :] = sin_hi
    d[256:384, :] = cos_lo
    d[384:512, :] = sin_lo

    point = lax.broadcasted_iota(jnp.int32, (1, PTS), 1)
    lane = lax.broadcasted_iota(jnp.int32, (WIN_ROWS, LANES), 1)

    def windows(c, win):
        @pl.when(c + 4 < NCHUNK)
        def _():
            for copy in fetch(c + 4):
                copy.start()

        for copy in fetch(c):
            copy.wait()
        for n in range(CHUNK):
            b = c * CHUNK + n
            live = point < counts[b]
            rows = theta[b].astype(F32)
            parts = []
            for x in range(2):
                own = jnp.where(live, values[x, pl.ds(b, 1), :], 0.0)
                parts.append((rows * own).astype(BF16))
            win[n] = nt_dot(jnp.concatenate(parts, 0), phi[b])

    def place(c, win):
        for n in range(CHUNK):
            b = c * CHUNK + n
            row = theta_offs[b]
            col = phi_offs[b]
            tile = col // LANES
            shift = col % LANES
            near = lane >= shift
            here = pl.ds(row, WIN_ROWS)
            for x in range(2):
                moved = pltpu.roll(win[n, x * WIN_ROWS : (x + 1) * WIN_ROWS, :], shift, 1)
                ext[tile, x, here, :] += jnp.where(near, moved, 0.0)
                ext[tile + 1, x, here, :] += jnp.where(near, 0.0, moved)

    for copy in small[2:]:
        copy.wait()
    windows(0, win_a)

    def step(i, carry):
        windows(2 * i + 1, win_b)
        place(2 * i, win_a)
        windows(2 * i + 2, win_a)
        place(2 * i + 1, win_b)
        return carry

    lax.fori_loop(0, NCHUNK // 2 - 1, step, 0)
    windows(NCHUNK - 1, win_b)
    place(NCHUNK - 2, win_a)
    place(NCHUNK - 1, win_b)

    for k in range(3):
        cols = slice(k * LANES, (k + 1) * LANES)
        for x in range(2):
            for t1 in range(T1):
                at = t1 * LANES + x * T0
                out[at : at + T0, cols] = ext[k, x, t1 * T0 : (t1 + 1) * T0, :].astype(BF16)
            at = T1 * LANES + x * T0
            out[at : at + 32, cols] = ext[k, x, ROWS_DEV:EXT_ROWS, :].astype(BF16)
            out[at + 32 : at + 64, cols] = jnp.zeros((32, LANES), BF16)


def spread(point_values, theta_weights, phi_weights, block_counts, theta_offsets, phi_offsets):
    base, rot = (jnp.asarray(table) for table in tables()[:2])
    vmem = pl.BlockSpec(memory_space=pltpu.VMEM)
    operands = [block_counts, theta_offsets, phi_offsets, base, rot, point_values, theta_weights, phi_weights]
    return pl.pallas_call(
        spread_kernel,
        out_shape=(
            jax.ShapeDtypeStruct((G_ROWS, EXT_COLS), BF16),
            jax.ShapeDtypeStruct((4 * ORDERS, EXT_COLS), BF16),
        ),
        in_specs=[pl.BlockSpec(memory_space=pltpu.HBM)] * len(operands),
        out_specs=(vmem, vmem),
        scratch_shapes=[
            pltpu.SMEM((BLOCKS,), jnp.int32),
            pltpu.SMEM((BLOCKS,), jnp.int32),
            pltpu.SMEM((BLOCKS,), jnp.int32),
            pltpu.VMEM((2 * ORDERS, EXT_COLS), F32),
            pltpu.VMEM((ORDERS, LANES), F32),
            pltpu.VMEM((2, BLOCKS, PTS), F32),
            pltpu.VMEM((BLOCKS, WIN_ROWS, PTS), BF16),
            pltpu.VMEM((BLOCKS, WIN_COLS, PTS), BF16),
            pltpu.VMEM((CHUNK, 2 * WIN_ROWS, WIN_COLS), F32),
            pltpu.VMEM((CHUNK, 2 * WIN_ROWS, WIN_COLS), F32),
            pltpu.VMEM((4, 2, EXT_ROWS, LANES), F32),
            pltpu.SemaphoreType.DMA((2, NCHUNK)),
            pltpu.SemaphoreType.DMA((6,)),
        ],
        compiler_params=pltpu.CompilerParams(vmem_limit_bytes=24 * MIB),
        name="spread",
    )(*(pltpu.with_memory_space_constraint(operand, pltpu.HBM) for operand in operands))


def split(value):
    hi = value.astype(BF16)
    return hi, (value - hi.astype(F32)).astype(BF16)


def finish_kernel(
    g, d, first_hbm, twiddle_hbm, second_hbm, conv_hbm, out, conv,
    a, b, got_a, got_b, relay_a, relay_b, on_a, on_b, sum_a, sum_b, got_a2, got_b2,
    q, qz_a, qz_b, r_a, r_b, first, twiddle, second,
    conv_sem, send_a, recv_a, send_b, recv_b, send_a2, recv_a2, send_b2, recv_b2, send_z, recv_z,
):
    lat = lax.axis_index("lat")
    lon = lax.axis_index("lon")
    z_lo = lon // 16
    my = lon // 4 % 4
    mx = lon % 4
    zc = lat * 2 + z_lo

    def x_peer(by):
        to = lax.rem(mx + by, NX)
        return to, (lat, z_lo * 16 + my * 4 + to)

    def y_peer(by):
        to = lax.rem(my + by, NY)
        return to, (lat, z_lo * 16 + to * 4 + mx)

    def z_peer(by):
        to = lax.rem(zc + by, NZC)
        return to, (to // 2, to % 2 * 16 + my * 4 + mx)

    barrier = pltpu.get_barrier_semaphore()
    for peer, count in ((x_peer, NX), (y_peer, NY), (z_peer, NZC)):
        for by in range(1, count):
            pl.semaphore_signal(barrier, inc=1, device_id=peer(by)[1], device_id_type=MESH)

    half = T1 * LANES // 2
    conv_loads = [
        pltpu.make_async_copy(conv_hbm.at[0, pl.ds(k * 1024, 1024)], conv.at[0, pl.ds(k * 1024, 1024)], conv_sem.at[k])
        for k in range(4)
    ]
    table_loads = [
        pltpu.make_async_copy(source, dest, conv_sem.at[4 + k])
        for k, (source, dest) in enumerate(((first_hbm, first), (twiddle_hbm, twiddle), (second_hbm, second)))
    ]
    for copy in table_loads:
        copy.start()
    for copy in conv_loads:
        copy.start()

    early = lax.broadcasted_iota(jnp.int32, (ORDERS, LANES), 1) < 64

    def along(product, at):
        cut = slice(at * LANES, (at + 1) * LANES)
        by_cos = product[0:128, cut] + product[256:384, cut]
        by_sin = pltpu.roll(product[128:256, cut] + product[384:512, cut], 64, 1)
        return (by_cos + jnp.where(early, by_sin, -by_sin)).reshape(NX, NY, NZC, LANES)

    for pair in range(4):
        product = nt_dot(d[...], g[pair * 256 : pair * 256 + 256, :])
        for at in range(2):
            a[:, :, pair * 2 + at, :, :] = along(product, at)
    for pair in range(4):
        product = nt_dot(d[...], g[half + pair * 256 : half + pair * 256 + 256, :])
        for at in range(2):
            b[:, :, pair * 2 + at, :, :] = along(product, at)
    b[:, :, 8, :, :] = along(nt_dot(d[...], g[T1 * LANES : G_ROWS, :]), 0)
    pl.semaphore_wait(barrier, (NX - 1) + (NY - 1) + (NZC - 1))

    def ring(part, peer, relay, on, got, send, recv):
        (ahead, ahead_id), (across, _), (behind, behind_id) = peer(1), peer(2), peer(3)

        def copy(k, source, dest, device):
            return pltpu.make_async_remote_copy(
                src_ref=source, dst_ref=dest, send_sem=send.at[k], recv_sem=recv.at[k],
                device_id=device, device_id_type=MESH,
            )

        low, high = pl.ds(0, 2), pl.ds(2, 2)
        copies = [
            copy(0, part(across, low), relay.at[0], ahead_id),
            copy(1, part(across, high), relay.at[1], behind_id),
            copy(2, part(ahead, high), got.at[0, high], ahead_id),
            copy(3, part(behind, low), got.at[1, low], behind_id),
            copy(4, on.at[0], got.at[0, low], ahead_id),
            copy(5, on.at[1], got.at[1, high], behind_id),
        ]
        for one in copies[:4]:
            one.start()

        def pass_on():
            copies[0].wait_recv()
            on[0] = part(ahead, low)[...] + relay[0]
            copies[4].start()
            copies[1].wait_recv()
            on[1] = part(behind, high)[...] + relay[1]
            copies[5].start()

        return copies, pass_on

    copies_a, pass_on_a = ring(lambda to, side: a.at[to, side], x_peer, relay_a, on_a, got_a, send_a, recv_a)
    copies_b, pass_on_b = ring(lambda to, side: b.at[side, to], y_peer, relay_b, on_b, got_b, send_b, recv_b)
    pass_on_a()
    pass_on_b()

    def exchange(source, dest, peer, send, recv):
        copies = []
        for by in range(1, 4):
            to, device = peer(by)
            copies.append(pltpu.make_async_remote_copy(
                src_ref=source.at[to], dst_ref=dest.at[by - 1], send_sem=send.at[by - 1], recv_sem=recv.at[by - 1],
                device_id=device, device_id_type=MESH,
            ))
        for copy in copies:
            copy.start()
        return copies

    for copy in copies_a[2:]:
        copy.wait_recv()
    sum_a[...] = a[mx] + got_a[0] + got_a[1]
    copies_a2 = exchange(sum_a, got_a2, y_peer, send_a2, recv_a2)
    for copy in copies_b[2:]:
        copy.wait_recv()
    sum_b[...] = b[:, my] + got_b[0] + got_b[1]
    copies_b2 = exchange(sum_b, got_b2, x_peer, send_b2, recv_b2)

    def deliver(source, dest, row):
        copies = []
        for by in range(1, NZC):
            to, device = z_peer(by)
            copies.append(pltpu.make_async_remote_copy(
                src_ref=source.at[to], dst_ref=dest.at[zc],
                send_sem=send_z.at[row, by - 1], recv_sem=recv_z.at[row, by - 1],
                device_id=device, device_id_type=MESH,
            ))
        for copy in copies:
            copy.start()
        dest[zc] = source[zc]
        return copies

    q[17 * 8 :, :] = jnp.zeros((7 * 8, LANES), F32)
    for copy in copies_a2:
        copy.wait_recv()
    q[0:64, :] = ((sum_a[my] + got_a2[0]) + (got_a2[1] + got_a2[2])).reshape(64, LANES)
    for z in range(NZC):
        qz_a[z] = q[pl.ds(z, 8, stride=8), :]
    copies_za = deliver(qz_a, r_a, 0)
    for copy in copies_b2:
        copy.wait_recv()
    q[64:136, :] = ((sum_b[mx] + got_b2[0]) + (got_b2[1] + got_b2[2])).reshape(72, LANES)
    for z in range(NZC):
        qz_b[z] = q[pl.ds(64 + z, 16, stride=8), :]
    copies_zb = deliver(qz_b, r_b, 1)
    for copy in copies_za + copies_zb:
        copy.wait_recv()

    for copy in table_loads:
        copy.wait()
    later = [r_b[2 * i] + r_b[2 * i + 1] for i in range(4)]
    top = lax.broadcasted_iota(jnp.int32, (T1, LANES), 0) == 0
    rows = [
        jnp.concatenate([r_a[2 * i] + r_a[2 * i + 1], later[i][0:8, :]], 0)
        + jnp.where(top, jnp.broadcast_to(later[i - 1][8:9, :], (T1, LANES)), 0.0)
        for i in range(4)
    ]
    hi, lo = split(jnp.concatenate(rows, 0))
    both = jnp.dot(first[...], jnp.concatenate([hi, hi, lo, jnp.zeros_like(hi)], 0), preferred_element_type=F32)
    by_sin = pltpu.roll(both[64:128], 64, 1)
    inner = both[0:64] + jnp.where(early[0:64], by_sin, -by_sin)
    turned = inner * twiddle[0] + pltpu.roll(inner, 64, 1) * twiddle[1]
    hi, lo = split(turned)
    parts = nt_dot(second[...], jnp.concatenate([hi, hi, lo], 1))
    hi, lo = split(jnp.concatenate([parts[32 * j : 32 * j + 32] for j in range(4)], 1))
    for side in range(2):
        cut = slice(side * LANES, (side + 1) * LANES)
        out[side, 0:32, :] = hi[:, cut].astype(F32)
        out[side, 32:64, :] = lo[:, cut].astype(F32)

    for copy in conv_loads:
        copy.wait()
    for group in (copies_a, copies_b, copies_a2, copies_b2, copies_za, copies_zb):
        for copy in group:
            copy.wait_send()


def finish(g, d, conversion):
    first, twiddle, second = (jnp.asarray(table) for table in tables()[2:])
    vmem = pl.BlockSpec(memory_space=pltpu.VMEM)
    dma = pltpu.SemaphoreType.DMA
    return pl.pallas_call(
        finish_kernel,
        out_shape=(
            jax.ShapeDtypeStruct((2, 64, LANES), F32),
            jax.ShapeDtypeStruct((1, GRID_ROWS, DEGREES), BF16),
        ),
        in_specs=[vmem, vmem] + [pl.BlockSpec(memory_space=pltpu.HBM)] * 4,
        out_specs=(vmem, vmem),
        scratch_shapes=[
            pltpu.VMEM((NX, NY, 8, NZC, LANES), F32),
            pltpu.VMEM((NX, NY, 9, NZC, LANES), F32),
            pltpu.VMEM((2, NY, 8, NZC, LANES), F32),
            pltpu.VMEM((2, NX, 9, NZC, LANES), F32),
            pltpu.VMEM((2, 2, 8, NZC, LANES), F32),
            pltpu.VMEM((2, 2, 9, NZC, LANES), F32),
            pltpu.VMEM((2, 2, 8, NZC, LANES), F32),
            pltpu.VMEM((2, 2, 9, NZC, LANES), F32),
            pltpu.VMEM((NY, 8, NZC, LANES), F32),
            pltpu.VMEM((NX, 9, NZC, LANES), F32),
            pltpu.VMEM((3, 8, NZC, LANES), F32),
            pltpu.VMEM((3, 9, NZC, LANES), F32),
            pltpu.VMEM((24 * 8, LANES), F32),
            pltpu.VMEM((NZC, 8, LANES), F32),
            pltpu.VMEM((NZC, 16, LANES), F32),
            pltpu.VMEM((NZC, 8, LANES), F32),
            pltpu.VMEM((NZC, 16, LANES), F32),
            pltpu.VMEM((128, 256), BF16),
            pltpu.VMEM((2, 64, LANES), F32),
            pltpu.VMEM((128, 384), BF16),
            dma((7,)),
            dma((6,)), dma((6,)), dma((6,)), dma((6,)),
            dma((3,)), dma((3,)), dma((3,)), dma((3,)),
            dma((2, 7)), dma((2, 7)),
        ],
        compiler_params=pltpu.CompilerParams(
            collective_id=0, has_side_effects=True, vmem_limit_bytes=20 * MIB
        ),
        name="finish",
    )(g, d, *(pltpu.with_memory_space_constraint(operand, pltpu.HBM) for operand in (first, twiddle, second, conversion)))


def convert_kernel(spec, conv, out):
    total = jnp.zeros((4, DEGREES), F32)
    for block in range(16):
        here = pl.ds((block + 8) % 16, 4, stride=16)
        rows = jnp.concatenate([spec[0, here, :], spec[1, here, :]], 1).astype(BF16)
        part = conv[0, block * 256 : block * 256 + 256, :]
        total += jnp.dot(rows, part, preferred_element_type=F32)
    out[0] = total[0:2] + total[2:4]


def convert(spec, conversion):
    vmem = pl.BlockSpec(memory_space=pltpu.VMEM)
    return pl.pallas_call(
        convert_kernel,
        out_shape=jax.ShapeDtypeStruct((1, 2, DEGREES), F32),
        in_specs=[vmem, vmem],
        out_specs=vmem,
        compiler_params=pltpu.CompilerParams(vmem_limit_bytes=24 * MIB),
        name="convert",
    )(spec, conversion)


def shards(
    point_values, theta_weights, phi_weights, block_counts, theta_offsets, phi_offsets, conversion
):
    g, d = spread(point_values, theta_weights, phi_weights, block_counts, theta_offsets, phi_offsets)
    return convert(*finish(g, d, conversion))


def solution(mesh):
    placed = (
        P(None, ("lat", "lon"), None),
        P(("lat", "lon"), None, None),
        P(("lat", "lon"), None, None),
        P(("lat", "lon")),
        P(("lat", "lon")),
        P(("lat", "lon")),
        P(("lat", "lon"), None, None),
    )
    return jax.shard_map(
        shards, mesh=mesh, in_specs=placed, out_specs=P(("lat", "lon"), None, None), check_vma=False
    )
```

```python
import functools
import math

import jax
import jax.numpy as jnp
import numpy as np
from jax import lax
from jax.experimental import pallas as pl
from jax.experimental.pallas import tpu as pltpu
from jax.sharding import PartitionSpec as P

GRID_ROWS = 4096
GRID_COLS = 8192
ORDERS = 128
BLOCKS = 64
WIN_ROWS = 32
WIN_COLS = 128
PTS = 256
ROWS_DEV = 1024
COLS_DEV = 256
EXT_ROWS = ROWS_DEV + WIN_ROWS
EXT_COLS = COLS_DEV + WIN_COLS
DEGREES = 2048
LANES = 128
T0 = 64
T1 = ROWS_DEV // T0
NX, NY, NZC = 4, 4, 8
CHUNK = 16
NCHUNK = BLOCKS // CHUNK
G_ROWS = T1 * LANES + LANES
MESH = pl.DeviceIdType.MESH
MIB = 1 << 20
BF16 = jnp.bfloat16
F32 = jnp.float32


def split_np(table):
    hi = table.astype(jnp.bfloat16)
    lo = (table - hi.astype(np.float64)).astype(jnp.bfloat16)
    return hi, lo


@functools.cache
def tables():
    place = np.arange(ORDERS)
    gx, gy, zc = place // 32, place // 8 % 4, place % 8
    order = zc * 16 + gy * 4 + gx - ORDERS // 2
    phase = (order[:, None] * np.arange(EXT_COLS)[None, :]) % GRID_COLS * (2 * np.pi / GRID_COLS)
    base = np.concatenate([np.cos(phase), np.sin(phase)]).astype(np.float32)
    turn = (order[:, None] * np.arange(32)[None, :]) % 32 * (2 * np.pi / 32)
    rot = np.zeros((2 * ORDERS, LANES), np.float32)
    rot[:ORDERS, :32] = np.cos(turn)
    rot[:ORDERS, 32:64] = np.sin(turn)
    base = np.concatenate([base, rot], 1)

    index = np.arange(64)
    angle = index[:, None] * index[None, :] % 64 * (2 * np.pi / 64)
    cos, sin = np.cos(angle), np.sin(angle)
    hi, lo = split_np(np.concatenate([cos, sin]))
    first = np.concatenate([hi, lo, hi, np.zeros_like(hi)], 1)
    unitary = 1.0 / math.sqrt(GRID_ROWS * GRID_COLS)
    angle = index[:, None] * index[None, :] * (2 * np.pi / 4096)
    twiddle = np.stack([
        np.concatenate([np.cos(angle), np.cos(angle)], 1), np.concatenate([np.sin(angle), -np.sin(angle)], 1)
    ])
    twiddle = (twiddle * unitary).astype(np.float32)
    second = np.block([[cos, sin], [-sin, cos]]).reshape(2, 16, 4, 128).transpose(2, 0, 1, 3).reshape(128, 128)
    hi, lo = split_np(second)
    second = np.concatenate([hi, lo, hi], 1)
    return base, first, twiddle, second


def nt_dot(a, b):
    return lax.dot_general(a, b, (((1,), (1,)), ((), ())), preferred_element_type=F32)


def spread_kernel(
    counts_hbm, theta_offs_hbm, phi_offs_hbm, base_hbm, values_hbm, theta_hbm, phi_hbm, out, d,
    counts, theta_offs, phi_offs, base, values, theta, phi, win_a, win_b, ext, sems, small_sems,
):
    small = [
        pltpu.make_async_copy(source, dest, small_sems.at[k])
        for k, (source, dest) in enumerate((
            (base_hbm, base), (counts_hbm, counts), (values_hbm, values),
            (theta_offs_hbm, theta_offs), (phi_offs_hbm, phi_offs),
        ))
    ]
    for copy in small:
        copy.start()

    def fetch(c):
        part = pl.ds(c * CHUNK, CHUNK)
        return (
            pltpu.make_async_copy(theta_hbm.at[part], theta.at[part], sems.at[0, c]),
            pltpu.make_async_copy(phi_hbm.at[part], phi.at[part], sems.at[1, c]),
        )

    for c in range(3):
        for copy in fetch(c):
            copy.start()

    def clear(i, carry):
        for k in range(4):
            for x in range(2):
                ext[k, x, pl.ds(pl.multiple_of(i * 96, 8), 96), :] = jnp.zeros((96, LANES), F32)
        return carry

    lax.fori_loop(0, EXT_ROWS // 96, clear, 0)

    small[0].wait()
    lon = lax.axis_index("lon")
    place_of = lax.broadcasted_iota(jnp.int32, (ORDERS, LANES), 1)
    turn = base[:ORDERS, EXT_COLS:]
    turn_cos = jnp.sum(jnp.where(place_of == lon, turn, 0.0), axis=1, keepdims=True)
    turn_sin = jnp.sum(jnp.where(place_of == lon + 32, turn, 0.0), axis=1, keepdims=True)
    cos, sin = base[:ORDERS, :EXT_COLS], base[ORDERS:, :EXT_COLS]
    cos_hi, cos_lo = split(cos * turn_cos - sin * turn_sin)
    sin_hi, sin_lo = split(sin * turn_cos + cos * turn_sin)
    d[0:128, :] = cos_hi
    d[128:256, :] = sin_hi
    d[256:384, :] = cos_lo
    d[384:512, :] = sin_lo

    point = lax.broadcasted_iota(jnp.int32, (1, PTS), 1)
    lane = lax.broadcasted_iota(jnp.int32, (WIN_ROWS, LANES), 1)

    def windows(c, win):
        @pl.when(c + 3 < NCHUNK)
        def _():
            for copy in fetch(c + 3):
                copy.start()

        for copy in fetch(c):
            copy.wait()
        for n in range(CHUNK):
            b = c * CHUNK + n
            live = point < counts[b]
            rows = theta[b].astype(F32)
            parts = []
            for x in range(2):
                own = jnp.where(live, values[x, pl.ds(b, 1), :], 0.0)
                parts.append((rows * own).astype(BF16))
            win[n] = nt_dot(jnp.concatenate(parts, 0), phi[b])

    def place(c, win):
        for n in range(CHUNK):
            b = c * CHUNK + n
            row = theta_offs[b]
            col = phi_offs[b]
            tile = col // LANES
            shift = col % LANES
            near = lane >= shift
            here = pl.ds(row, WIN_ROWS)
            for x in range(2):
                moved = pltpu.roll(win[n, x * WIN_ROWS : (x + 1) * WIN_ROWS, :], shift, 1)
                ext[tile, x, here, :] += jnp.where(near, moved, 0.0)
                ext[tile + 1, x, here, :] += jnp.where(near, 0.0, moved)

    for copy in small[1:]:
        copy.wait()
    windows(0, win_a)

    def step(i, carry):
        windows(2 * i + 1, win_b)
        place(2 * i, win_a)
        windows(2 * i + 2, win_a)
        place(2 * i + 1, win_b)
        return carry

    lax.fori_loop(0, NCHUNK // 2 - 1, step, 0)
    windows(NCHUNK - 1, win_b)
    place(NCHUNK - 2, win_a)
    place(NCHUNK - 1, win_b)

    for k in range(3):
        cols = slice(k * LANES, (k + 1) * LANES)
        for x in range(2):
            for t1 in range(T1):
                at = t1 * LANES + x * T0
                out[at : at + T0, cols] = ext[k, x, t1 * T0 : (t1 + 1) * T0, :].astype(BF16)
            at = T1 * LANES + x * T0
            out[at : at + 32, cols] = ext[k, x, ROWS_DEV:EXT_ROWS, :].astype(BF16)
            out[at + 32 : at + 64, cols] = jnp.zeros((32, LANES), BF16)


def spread(point_values, theta_weights, phi_weights, block_counts, theta_offsets, phi_offsets):
    base = jnp.asarray(tables()[0])
    vmem = pl.BlockSpec(memory_space=pltpu.VMEM)
    operands = [block_counts, theta_offsets, phi_offsets, base, point_values, theta_weights, phi_weights]
    return pl.pallas_call(
        spread_kernel,
        out_shape=(
            jax.ShapeDtypeStruct((G_ROWS, EXT_COLS), BF16),
            jax.ShapeDtypeStruct((4 * ORDERS, EXT_COLS), BF16),
        ),
        in_specs=[pl.BlockSpec(memory_space=pltpu.HBM)] * len(operands),
        out_specs=(vmem, vmem),
        scratch_shapes=[
            pltpu.SMEM((BLOCKS,), jnp.int32),
            pltpu.SMEM((BLOCKS,), jnp.int32),
            pltpu.SMEM((BLOCKS,), jnp.int32),
            pltpu.VMEM((2 * ORDERS, EXT_COLS + LANES), F32),
            pltpu.VMEM((2, BLOCKS, PTS), F32),
            pltpu.VMEM((BLOCKS, WIN_ROWS, PTS), BF16),
            pltpu.VMEM((BLOCKS, WIN_COLS, PTS), BF16),
            pltpu.VMEM((CHUNK, 2 * WIN_ROWS, WIN_COLS), F32),
            pltpu.VMEM((CHUNK, 2 * WIN_ROWS, WIN_COLS), F32),
            pltpu.VMEM((4, 2, EXT_ROWS, LANES), F32),
            pltpu.SemaphoreType.DMA((2, NCHUNK)),
            pltpu.SemaphoreType.DMA((5,)),
        ],
        compiler_params=pltpu.CompilerParams(vmem_limit_bytes=24 * MIB),
        name="spread",
    )(*(pltpu.with_memory_space_constraint(operand, pltpu.HBM) for operand in operands))


def split(value):
    hi = value.astype(BF16)
    return hi, (value - hi.astype(F32)).astype(BF16)


def finish_kernel(
    g, d, first_hbm, twiddle_hbm, second_hbm, conv_hbm, out, conv,
    a, b, got_a, got_b, relay_a, relay_b, on_a, on_b, sum_a, sum_b, got_a2, got_b2,
    q, qz_a, qz_b, r_a, r_b, first, twiddle, second,
    conv_sem, send_a, recv_a, send_b, recv_b, send_a2, recv_a2, send_b2, recv_b2, send_z, recv_z,
):
    lat = lax.axis_index("lat")
    lon = lax.axis_index("lon")
    z_lo = lon // 16
    my = lon // 4 % 4
    mx = lon % 4
    zc = lat * 2 + z_lo

    def x_peer(by):
        to = lax.rem(mx + by, NX)
        return to, (lat, z_lo * 16 + my * 4 + to)

    def y_peer(by):
        to = lax.rem(my + by, NY)
        return to, (lat, z_lo * 16 + to * 4 + mx)

    def z_peer(by):
        to = lax.rem(zc + by, NZC)
        return to, (to // 2, to % 2 * 16 + my * 4 + mx)

    barrier = pltpu.get_barrier_semaphore()
    far_first = [(z_peer, by) for by in (4, 3, 5, 1, 7, 2, 6)] + [(peer, by) for by in (2, 1, 3) for peer in (x_peer, y_peer)]
    for peer, by in far_first:
        pl.semaphore_signal(barrier, inc=1, device_id=peer(by)[1], device_id_type=MESH)

    half = T1 * LANES // 2
    conv_loads = [
        pltpu.make_async_copy(conv_hbm.at[0, pl.ds(k * 1024, 1024)], conv.at[0, pl.ds(k * 1024, 1024)], conv_sem.at[k])
        for k in range(4)
    ]
    table_loads = [
        pltpu.make_async_copy(source, dest, conv_sem.at[4 + k])
        for k, (source, dest) in enumerate(((first_hbm, first), (twiddle_hbm, twiddle), (second_hbm, second)))
    ]
    for copy in table_loads:
        copy.start()
    for copy in conv_loads:
        copy.start()

    early = lax.broadcasted_iota(jnp.int32, (ORDERS, LANES), 1) < 64

    def along(product, at):
        cut = slice(at * LANES, (at + 1) * LANES)
        by_cos = product[0:128, cut] + product[256:384, cut]
        by_sin = pltpu.roll(product[128:256, cut] + product[384:512, cut], 64, 1)
        return (by_cos + jnp.where(early, by_sin, -by_sin)).reshape(NX, NY, NZC, LANES)

    for pair in range(4):
        product = nt_dot(d[...], g[pair * 256 : pair * 256 + 256, :])
        for at in range(2):
            a[:, :, pair * 2 + at, :, :] = along(product, at)
    for pair in range(4):
        product = nt_dot(d[...], g[half + pair * 256 : half + pair * 256 + 256, :])
        for at in range(2):
            b[:, :, pair * 2 + at, :, :] = along(product, at)
    a[:, :, 8, :, :] = along(nt_dot(d[...], g[T1 * LANES : G_ROWS, :]), 0)
    pl.semaphore_wait(barrier, (NX - 1) + (NY - 1) + (NZC - 1))

    def ring(part, peer, relay, on, got, send, recv):
        (ahead, ahead_id), (across, _), (behind, behind_id) = peer(1), peer(2), peer(3)

        def copy(k, source, dest, device):
            return pltpu.make_async_remote_copy(
                src_ref=source, dst_ref=dest, send_sem=send.at[k], recv_sem=recv.at[k],
                device_id=device, device_id_type=MESH,
            )

        low, high = pl.ds(0, 2), pl.ds(2, 2)
        copies = [
            copy(0, part(across, low), relay.at[0], ahead_id),
            copy(1, part(across, high), relay.at[1], behind_id),
            copy(2, part(ahead, high), got.at[0, high], ahead_id),
            copy(3, part(behind, low), got.at[1, low], behind_id),
            copy(4, on.at[0], got.at[0, low], ahead_id),
            copy(5, on.at[1], got.at[1, high], behind_id),
        ]
        def pass_on():
            copies[0].wait_recv()
            on[0] = part(ahead, low)[...] + relay[0]
            copies[4].start()
            copies[1].wait_recv()
            on[1] = part(behind, high)[...] + relay[1]
            copies[5].start()

        return copies, pass_on

    copies_a, pass_on_a = ring(lambda to, side: a.at[to, side], x_peer, relay_a, on_a, got_a, send_a, recv_a)
    copies_b, pass_on_b = ring(lambda to, side: b.at[side, to], y_peer, relay_b, on_b, got_b, send_b, recv_b)
    for one in copies_a[:2] + copies_b[:2] + copies_a[2:4] + copies_b[2:4]:
        one.start()
    pass_on_a()
    pass_on_b()

    def exchange(source, dest, peer, send, recv):
        copies = []
        for by in range(1, 4):
            to, device = peer(by)
            copies.append(pltpu.make_async_remote_copy(
                src_ref=source.at[to], dst_ref=dest.at[by - 1], send_sem=send.at[by - 1], recv_sem=recv.at[by - 1],
                device_id=device, device_id_type=MESH,
            ))
        for copy in copies:
            copy.start()
        return copies

    for copy in copies_a[2:]:
        copy.wait_recv()
    sum_a[...] = a[mx] + got_a[0] + got_a[1]
    copies_a2 = exchange(sum_a, got_a2, y_peer, send_a2, recv_a2)
    for copy in copies_b[2:]:
        copy.wait_recv()
    sum_b[...] = b[:, my] + got_b[0] + got_b[1]
    copies_b2 = exchange(sum_b, got_b2, x_peer, send_b2, recv_b2)

    def deliver(source, dest, row):
        copies = []
        for by in range(1, NZC):
            to, device = z_peer(by)
            copies.append(pltpu.make_async_remote_copy(
                src_ref=source.at[to], dst_ref=dest.at[zc],
                send_sem=send_z.at[row, by - 1], recv_sem=recv_z.at[row, by - 1],
                device_id=device, device_id_type=MESH,
            ))
        for copy in copies:
            copy.start()
        dest[zc] = source[zc]
        return copies

    q[72:128, :] = jnp.zeros((56, LANES), F32)
    for copy in copies_a2:
        copy.wait_recv()
    q[0:72, :] = ((sum_a[my] + got_a2[0]) + (got_a2[1] + got_a2[2])).reshape(72, LANES)
    for z in range(NZC):
        qz_a[z] = q[pl.ds(z, 16, stride=8), :]
    copies_za = deliver(qz_a, r_a, 0)
    for copy in copies_b2:
        copy.wait_recv()
    q[128:192, :] = ((sum_b[mx] + got_b2[0]) + (got_b2[1] + got_b2[2])).reshape(64, LANES)
    for z in range(NZC):
        qz_b[z] = q[pl.ds(128 + z, 8, stride=8), :]
    copies_zb = deliver(qz_b, r_b, 1)
    for copy in copies_za + copies_zb:
        copy.wait_recv()

    for copy in table_loads:
        copy.wait()
    first_rows = [r_a[2 * i] + r_a[2 * i + 1] for i in range(4)]
    top = lax.broadcasted_iota(jnp.int32, (T1, LANES), 0) == 0
    rows = [
        jnp.concatenate([first_rows[i][0:8, :], r_b[2 * i] + r_b[2 * i + 1]], 0)
        + jnp.where(top, jnp.broadcast_to(first_rows[i - 1][8:9, :], (T1, LANES)), 0.0)
        for i in range(4)
    ]
    hi, lo = split(jnp.concatenate(rows, 0))
    both = jnp.dot(first[...], jnp.concatenate([hi, hi, lo, jnp.zeros_like(hi)], 0), preferred_element_type=F32)
    by_sin = pltpu.roll(both[64:128], 64, 1)
    inner = both[0:64] + jnp.where(early[0:64], by_sin, -by_sin)
    turned = inner * twiddle[0] + pltpu.roll(inner, 64, 1) * twiddle[1]
    hi, lo = split(turned)
    parts = nt_dot(second[...], jnp.concatenate([hi, hi, lo], 1))
    hi, lo = split(jnp.concatenate([parts[32 * j : 32 * j + 32] for j in range(4)], 1))
    for side in range(2):
        cut = slice(side * LANES, (side + 1) * LANES)
        out[side, 0:32, :] = hi[:, cut].astype(F32)
        out[side, 32:64, :] = lo[:, cut].astype(F32)

    for copy in conv_loads:
        copy.wait()
    for group in (copies_a, copies_b, copies_a2, copies_b2, copies_za, copies_zb):
        for copy in group:
            copy.wait_send()


def finish(g, d, conversion):
    first, twiddle, second = (jnp.asarray(table) for table in tables()[1:])
    vmem = pl.BlockSpec(memory_space=pltpu.VMEM)
    dma = pltpu.SemaphoreType.DMA
    return pl.pallas_call(
        finish_kernel,
        out_shape=(
            jax.ShapeDtypeStruct((2, 64, LANES), F32),
            jax.ShapeDtypeStruct((1, GRID_ROWS, DEGREES), BF16),
        ),
        in_specs=[vmem, vmem] + [pl.BlockSpec(memory_space=pltpu.HBM)] * 4,
        out_specs=(vmem, vmem),
        scratch_shapes=[
            pltpu.VMEM((NX, NY, 9, NZC, LANES), F32),
            pltpu.VMEM((NX, NY, 8, NZC, LANES), F32),
            pltpu.VMEM((2, NY, 9, NZC, LANES), F32),
            pltpu.VMEM((2, NX, 8, NZC, LANES), F32),
            pltpu.VMEM((2, 2, 9, NZC, LANES), F32),
            pltpu.VMEM((2, 2, 8, NZC, LANES), F32),
            pltpu.VMEM((2, 2, 9, NZC, LANES), F32),
            pltpu.VMEM((2, 2, 8, NZC, LANES), F32),
            pltpu.VMEM((NY, 9, NZC, LANES), F32),
            pltpu.VMEM((NX, 8, NZC, LANES), F32),
            pltpu.VMEM((3, 9, NZC, LANES), F32),
            pltpu.VMEM((3, 8, NZC, LANES), F32),
            pltpu.VMEM((24 * 8, LANES), F32),
            pltpu.VMEM((NZC, 16, LANES), F32),
            pltpu.VMEM((NZC, 8, LANES), F32),
            pltpu.VMEM((NZC, 16, LANES), F32),
            pltpu.VMEM((NZC, 8, LANES), F32),
            pltpu.VMEM((128, 256), BF16),
            pltpu.VMEM((2, 64, LANES), F32),
            pltpu.VMEM((128, 384), BF16),
            dma((7,)),
            dma((6,)), dma((6,)), dma((6,)), dma((6,)),
            dma((3,)), dma((3,)), dma((3,)), dma((3,)),
            dma((2, 7)), dma((2, 7)),
        ],
        compiler_params=pltpu.CompilerParams(
            collective_id=0, has_side_effects=True, vmem_limit_bytes=20 * MIB
        ),
        name="finish",
    )(g, d, *(pltpu.with_memory_space_constraint(operand, pltpu.HBM) for operand in (first, twiddle, second, conversion)))


def convert_kernel(spec, conv, out):
    total = jnp.zeros((4, DEGREES), F32)
    for block in range(16):
        here = pl.ds((block + 8) % 16, 4, stride=16)
        rows = jnp.concatenate([spec[0, here, :], spec[1, here, :]], 1).astype(BF16)
        part = conv[0, block * 256 : block * 256 + 256, :]
        total += jnp.dot(rows, part, preferred_element_type=F32)
    out[0] = total[0:2] + total[2:4]


def convert(spec, conversion):
    vmem = pl.BlockSpec(memory_space=pltpu.VMEM)
    return pl.pallas_call(
        convert_kernel,
        out_shape=jax.ShapeDtypeStruct((1, 2, DEGREES), F32),
        in_specs=[vmem, vmem],
        out_specs=vmem,
        compiler_params=pltpu.CompilerParams(vmem_limit_bytes=24 * MIB),
        name="convert",
    )(spec, conversion)


def shards(
    point_values, theta_weights, phi_weights, block_counts, theta_offsets, phi_offsets, conversion
):
    g, d = spread(point_values, theta_weights, phi_weights, block_counts, theta_offsets, phi_offsets)
    return convert(*finish(g, d, conversion))


def solution(mesh):
    placed = (
        P(None, ("lat", "lon"), None),
        P(("lat", "lon"), None, None),
        P(("lat", "lon"), None, None),
        P(("lat", "lon")),
        P(("lat", "lon")),
        P(("lat", "lon")),
        P(("lat", "lon"), None, None),
    )
    return jax.shard_map(
        shards, mesh=mesh, in_specs=placed, out_specs=P(("lat", "lon"), None, None), check_vma=False
    )
```

```python
import functools
import math

import jax
import jax.numpy as jnp
import numpy as np
from jax import lax
from jax.experimental import pallas as pl
from jax.experimental.pallas import tpu as pltpu
from jax.sharding import PartitionSpec as P

GRID_ROWS = 4096
GRID_COLS = 8192
ORDERS = 128
BLOCKS = 64
WIN_ROWS = 32
WIN_COLS = 128
PTS = 256
ROWS_DEV = 1024
COLS_DEV = 256
EXT_ROWS = ROWS_DEV + WIN_ROWS
EXT_COLS = COLS_DEV + WIN_COLS
DEGREES = 2048
LANES = 128
T0 = 64
T1 = ROWS_DEV // T0
NX, NY, NZC = 4, 4, 8
CHUNK = 16
NCHUNK = BLOCKS // CHUNK
G_ROWS = T1 * LANES + LANES
MESH = pl.DeviceIdType.MESH
MIB = 1 << 20
BF16 = jnp.bfloat16
F32 = jnp.float32


def split_np(table):
    hi = table.astype(jnp.bfloat16)
    lo = (table - hi.astype(np.float64)).astype(jnp.bfloat16)
    return hi, lo


@functools.cache
def tables():
    place = np.arange(ORDERS)
    gx, gy, zc = place // 32, place // 8 % 4, place % 8
    order = zc * 16 + gy * 4 + gx - ORDERS // 2
    phase = (order[:, None] * np.arange(EXT_COLS)[None, :]) % GRID_COLS * (2 * np.pi / GRID_COLS)
    base = np.concatenate([np.cos(phase), np.sin(phase)]).astype(np.float32)
    turn = (order[:, None] * np.arange(32)[None, :]) % 32 * (2 * np.pi / 32)
    rot = np.zeros((2 * ORDERS, LANES), np.float32)
    rot[:ORDERS, :32] = np.cos(turn)
    rot[:ORDERS, 32:64] = np.sin(turn)
    base = np.concatenate([base, rot], 1)

    index = np.arange(64)
    angle = index[:, None] * index[None, :] % 64 * (2 * np.pi / 64)
    cos, sin = np.cos(angle), np.sin(angle)
    hi, lo = split_np(np.concatenate([cos, sin]))
    first = np.concatenate([hi, lo, hi, np.zeros_like(hi)], 1)
    unitary = 1.0 / math.sqrt(GRID_ROWS * GRID_COLS)
    angle = index[:, None] * index[None, :] * (2 * np.pi / 4096)
    twiddle = np.stack([
        np.concatenate([np.cos(angle), np.cos(angle)], 1), np.concatenate([np.sin(angle), -np.sin(angle)], 1)
    ])
    twiddle = (twiddle * unitary).astype(np.float32)
    second = np.block([[cos, sin], [-sin, cos]]).reshape(2, 16, 4, 128).transpose(2, 0, 1, 3).reshape(128, 128)
    hi, lo = split_np(second)
    second = np.concatenate([hi, lo, hi], 1)
    return base, first, twiddle, second


def nt_dot(a, b):
    return lax.dot_general(a, b, (((1,), (1,)), ((), ())), preferred_element_type=F32)


def spread_kernel(
    counts_hbm, theta_offs_hbm, phi_offs_hbm, base_hbm, values_hbm, theta_hbm, phi_hbm, out, d,
    counts, theta_offs, phi_offs, base, values, theta, phi, win_a, win_b, ext, sems, small_sems,
):
    small = [
        pltpu.make_async_copy(source, dest, small_sems.at[k])
        for k, (source, dest) in enumerate((
            (base_hbm, base), (counts_hbm, counts), (values_hbm, values),
            (theta_offs_hbm, theta_offs), (phi_offs_hbm, phi_offs),
        ))
    ]
    for copy in small:
        copy.start()

    def fetch(c):
        part = pl.ds(c * CHUNK, CHUNK)
        return pltpu.make_async_copy(phi_hbm.at[part], phi.at[part], sems.at[0, c])

    def fetch_rows(k):
        part = (pl.ds(0, CHUNK), pl.ds(CHUNK, BLOCKS - CHUNK))[k]
        return pltpu.make_async_copy(theta_hbm.at[part], theta.at[part], sems.at[1, k])

    fetch_rows(0).start()
    fetch(0).start()
    fetch(1).start()
    fetch_rows(1).start()
    fetch(2).start()

    def clear(i, carry):
        for k in range(4):
            for x in range(2):
                ext[k, x, pl.ds(pl.multiple_of(i * 96, 8), 96), :] = jnp.zeros((96, LANES), F32)
        return carry

    lax.fori_loop(0, EXT_ROWS // 96, clear, 0)

    small[0].wait()
    lon = lax.axis_index("lon")
    place_of = lax.broadcasted_iota(jnp.int32, (ORDERS, LANES), 1)
    turn = base[:ORDERS, EXT_COLS:]
    turn_cos = jnp.sum(jnp.where(place_of == lon, turn, 0.0), axis=1, keepdims=True)
    turn_sin = jnp.sum(jnp.where(place_of == lon + 32, turn, 0.0), axis=1, keepdims=True)
    cos, sin = base[:ORDERS, :EXT_COLS], base[ORDERS:, :EXT_COLS]
    cos_hi, cos_lo = split(cos * turn_cos - sin * turn_sin)
    sin_hi, sin_lo = split(sin * turn_cos + cos * turn_sin)
    d[0:128, :] = cos_hi
    d[128:256, :] = sin_hi
    d[256:384, :] = cos_lo
    d[384:512, :] = sin_lo

    point = lax.broadcasted_iota(jnp.int32, (1, PTS), 1)
    lane = lax.broadcasted_iota(jnp.int32, (WIN_ROWS, LANES), 1)

    def windows(c, win):
        @pl.when(c + 3 < NCHUNK)
        def _():
            fetch(c + 3).start()

        fetch(c).wait()
        for n in range(CHUNK):
            b = c * CHUNK + n
            live = point < counts[b]
            rows = theta[b].astype(F32)
            parts = []
            for x in range(2):
                own = jnp.where(live, values[x, pl.ds(b, 1), :], 0.0)
                parts.append((rows * own).astype(BF16))
            win[n] = nt_dot(jnp.concatenate(parts, 0), phi[b])

    def place(c, win):
        for n in range(CHUNK):
            b = c * CHUNK + n
            row = theta_offs[b]
            col = phi_offs[b]
            tile = col // LANES
            shift = col % LANES
            near = lane >= shift
            here = pl.ds(row, WIN_ROWS)
            for x in range(2):
                moved = pltpu.roll(win[n, x * WIN_ROWS : (x + 1) * WIN_ROWS, :], shift, 1)
                ext[tile, x, here, :] += jnp.where(near, moved, 0.0)
                ext[tile + 1, x, here, :] += jnp.where(near, 0.0, moved)

    for copy in small[1:]:
        copy.wait()
    fetch_rows(0).wait()
    windows(0, win_a)
    fetch_rows(1).wait()

    def step(i, carry):
        windows(2 * i + 1, win_b)
        place(2 * i, win_a)
        windows(2 * i + 2, win_a)
        place(2 * i + 1, win_b)
        return carry

    lax.fori_loop(0, NCHUNK // 2 - 1, step, 0)
    windows(NCHUNK - 1, win_b)
    place(NCHUNK - 2, win_a)
    place(NCHUNK - 1, win_b)

    for k in range(3):
        cols = slice(k * LANES, (k + 1) * LANES)
        for x in range(2):
            for t1 in range(T1):
                at = t1 * LANES + x * T0
                out[at : at + T0, cols] = ext[k, x, t1 * T0 : (t1 + 1) * T0, :].astype(BF16)
            at = T1 * LANES + x * T0
            out[at : at + 32, cols] = ext[k, x, ROWS_DEV:EXT_ROWS, :].astype(BF16)
            out[at + 32 : at + 64, cols] = jnp.zeros((32, LANES), BF16)


def spread(point_values, theta_weights, phi_weights, block_counts, theta_offsets, phi_offsets):
    base = jnp.asarray(tables()[0])
    vmem = pl.BlockSpec(memory_space=pltpu.VMEM)
    operands = [block_counts, theta_offsets, phi_offsets, base, point_values, theta_weights, phi_weights]
    return pl.pallas_call(
        spread_kernel,
        out_shape=(
            jax.ShapeDtypeStruct((G_ROWS, EXT_COLS), BF16),
            jax.ShapeDtypeStruct((4 * ORDERS, EXT_COLS), BF16),
        ),
        in_specs=[pl.BlockSpec(memory_space=pltpu.HBM)] * len(operands),
        out_specs=(vmem, vmem),
        scratch_shapes=[
            pltpu.SMEM((BLOCKS,), jnp.int32),
            pltpu.SMEM((BLOCKS,), jnp.int32),
            pltpu.SMEM((BLOCKS,), jnp.int32),
            pltpu.VMEM((2 * ORDERS, EXT_COLS + LANES), F32),
            pltpu.VMEM((2, BLOCKS, PTS), F32),
            pltpu.VMEM((BLOCKS, WIN_ROWS, PTS), BF16),
            pltpu.VMEM((BLOCKS, WIN_COLS, PTS), BF16),
            pltpu.VMEM((CHUNK, 2 * WIN_ROWS, WIN_COLS), F32),
            pltpu.VMEM((CHUNK, 2 * WIN_ROWS, WIN_COLS), F32),
            pltpu.VMEM((4, 2, EXT_ROWS, LANES), F32),
            pltpu.SemaphoreType.DMA((2, NCHUNK)),
            pltpu.SemaphoreType.DMA((5,)),
        ],
        compiler_params=pltpu.CompilerParams(vmem_limit_bytes=24 * MIB),
        name="spread",
    )(*(pltpu.with_memory_space_constraint(operand, pltpu.HBM) for operand in operands))


def split(value):
    hi = value.astype(BF16)
    return hi, (value - hi.astype(F32)).astype(BF16)


def finish_kernel(
    g, d, first_hbm, twiddle_hbm, second_hbm, conv_hbm, out, conv,
    a, b, got_a, got_b, relay_a, relay_b, on_a, on_b, sum_a, sum_b, got_a2, got_b2,
    q, qz_a, qz_b, r_a, r_b, first, twiddle, second,
    conv_sem, send_a, recv_a, send_b, recv_b, send_a2, recv_a2, send_b2, recv_b2, send_z, recv_z,
):
    lat = lax.axis_index("lat")
    lon = lax.axis_index("lon")
    z_lo = lon // 16
    my = lon // 4 % 4
    mx = lon % 4
    zc = lat * 2 + z_lo

    def x_peer(by):
        to = lax.rem(mx + by, NX)
        return to, (lat, z_lo * 16 + my * 4 + to)

    def y_peer(by):
        to = lax.rem(my + by, NY)
        return to, (lat, z_lo * 16 + to * 4 + mx)

    def z_peer(by):
        to = lax.rem(zc + by, NZC)
        return to, (to // 2, to % 2 * 16 + my * 4 + mx)

    barrier = pltpu.get_barrier_semaphore()
    far_first = [(z_peer, by) for by in (4, 3, 5, 1, 7, 2, 6)] + [(peer, by) for by in (2, 1, 3) for peer in (x_peer, y_peer)]
    for peer, by in far_first:
        pl.semaphore_signal(barrier, inc=1, device_id=peer(by)[1], device_id_type=MESH)

    half = T1 * LANES // 2
    conv_loads = [
        pltpu.make_async_copy(conv_hbm, conv, conv_sem.at[k])
        for k in range(1)
    ]
    table_loads = [
        pltpu.make_async_copy(source, dest, conv_sem.at[4 + k])
        for k, (source, dest) in enumerate(((first_hbm, first), (twiddle_hbm, twiddle), (second_hbm, second)))
    ]
    for copy in table_loads:
        copy.start()
    for copy in conv_loads:
        copy.start()

    early = lax.broadcasted_iota(jnp.int32, (ORDERS, LANES), 1) < 64

    def along(product, at):
        cut = slice(at * LANES, (at + 1) * LANES)
        by_cos = product[0:128, cut] + product[256:384, cut]
        by_sin = pltpu.roll(product[128:256, cut] + product[384:512, cut], 64, 1)
        return (by_cos + jnp.where(early, by_sin, -by_sin)).reshape(NX, NY, NZC, LANES)

    for pair in range(4):
        product = nt_dot(d[...], g[pair * 256 : pair * 256 + 256, :])
        for at in range(2):
            a[:, :, pair * 2 + at, :, :] = along(product, at)
    for pair in range(4):
        product = nt_dot(d[...], g[half + pair * 256 : half + pair * 256 + 256, :])
        for at in range(2):
            b[:, :, pair * 2 + at, :, :] = along(product, at)
    a[:, :, 8, :, :] = along(nt_dot(d[...], g[T1 * LANES : G_ROWS, :]), 0)
    pl.semaphore_wait(barrier, (NX - 1) + (NY - 1) + (NZC - 1))

    def ring(part, peer, relay, on, got, send, recv):
        (ahead, ahead_id), (across, _), (behind, behind_id) = peer(1), peer(2), peer(3)

        def copy(k, source, dest, device):
            return pltpu.make_async_remote_copy(
                src_ref=source, dst_ref=dest, send_sem=send.at[k], recv_sem=recv.at[k],
                device_id=device, device_id_type=MESH,
            )

        low, high = pl.ds(0, 2), pl.ds(2, 2)
        copies = [
            copy(0, part(across, low), relay.at[0], ahead_id),
            copy(1, part(across, high), relay.at[1], behind_id),
            copy(2, part(ahead, high), got.at[0, high], ahead_id),
            copy(3, part(behind, low), got.at[1, low], behind_id),
            copy(4, on.at[0], got.at[0, low], ahead_id),
            copy(5, on.at[1], got.at[1, high], behind_id),
        ]
        def pass_on():
            copies[0].wait_recv()
            on[0] = part(ahead, low)[...] + relay[0]
            copies[4].start()
            copies[1].wait_recv()
            on[1] = part(behind, high)[...] + relay[1]
            copies[5].start()

        return copies, pass_on

    copies_a, pass_on_a = ring(lambda to, side: a.at[to, side], x_peer, relay_a, on_a, got_a, send_a, recv_a)
    copies_b, pass_on_b = ring(lambda to, side: b.at[side, to], y_peer, relay_b, on_b, got_b, send_b, recv_b)
    for one in copies_a[:2] + copies_b[:2] + copies_a[2:4] + copies_b[2:4]:
        one.start()
    pass_on_a()
    pass_on_b()

    def exchange(source, dest, peer, send, recv):
        copies = []
        for by in (2, 1, 3):
            to, device = peer(by)
            copies.append(pltpu.make_async_remote_copy(
                src_ref=source.at[to], dst_ref=dest.at[by - 1], send_sem=send.at[by - 1], recv_sem=recv.at[by - 1],
                device_id=device, device_id_type=MESH,
            ))
        for copy in copies:
            copy.start()
        return copies

    for copy in copies_a[2:]:
        copy.wait_recv()
    sum_a[...] = a[mx] + got_a[0] + got_a[1]
    copies_a2 = exchange(sum_a, got_a2, y_peer, send_a2, recv_a2)
    for copy in copies_b[2:]:
        copy.wait_recv()
    sum_b[...] = b[:, my] + got_b[0] + got_b[1]
    copies_b2 = exchange(sum_b, got_b2, x_peer, send_b2, recv_b2)

    def deliver(source, dest, row):
        copies = []
        for by in (4, 3, 5, 1, 7, 2, 6):
            to, device = z_peer(by)
            copies.append(pltpu.make_async_remote_copy(
                src_ref=source.at[to], dst_ref=dest.at[zc],
                send_sem=send_z.at[row, by - 1], recv_sem=recv_z.at[row, by - 1],
                device_id=device, device_id_type=MESH,
            ))
        for copy in copies:
            copy.start()
        dest[zc] = source[zc]
        return copies

    q[72:128, :] = jnp.zeros((56, LANES), F32)
    for copy in copies_a2:
        copy.wait_recv()
    q[0:72, :] = ((sum_a[my] + got_a2[0]) + (got_a2[1] + got_a2[2])).reshape(72, LANES)
    for z in range(NZC):
        qz_a[z] = q[pl.ds(z, 16, stride=8), :]
    copies_za = deliver(qz_a, r_a, 0)
    for copy in copies_b2:
        copy.wait_recv()
    q[128:192, :] = ((sum_b[mx] + got_b2[0]) + (got_b2[1] + got_b2[2])).reshape(64, LANES)
    for z in range(NZC):
        qz_b[z] = q[pl.ds(128 + z, 8, stride=8), :]
    copies_zb = deliver(qz_b, r_b, 1)
    for group in (copies_a, copies_b, copies_a2, copies_b2, copies_za):
        for copy in group:
            copy.wait_send()
    for copy in table_loads + conv_loads:
        copy.wait()
    for copy in copies_za + copies_zb:
        copy.wait_recv()

    first_rows = [r_a[2 * i] + r_a[2 * i + 1] for i in range(4)]
    top = lax.broadcasted_iota(jnp.int32, (T1, LANES), 0) == 0
    rows = [
        jnp.concatenate([first_rows[i][0:8, :], r_b[2 * i] + r_b[2 * i + 1]], 0)
        + jnp.where(top, jnp.broadcast_to(first_rows[i - 1][8:9, :], (T1, LANES)), 0.0)
        for i in range(4)
    ]
    hi, lo = split(jnp.concatenate(rows, 0))
    both = jnp.dot(first[...], jnp.concatenate([hi, hi, lo, jnp.zeros_like(hi)], 0), preferred_element_type=F32)
    by_sin = pltpu.roll(both[64:128], 64, 1)
    inner = both[0:64] + jnp.where(early[0:64], by_sin, -by_sin)
    turned = inner * twiddle[0] + pltpu.roll(inner, 64, 1) * twiddle[1]
    hi, lo = split(turned)
    parts = nt_dot(second[...], jnp.concatenate([hi, hi, lo], 1))
    hi, lo = split(jnp.concatenate([parts[32 * j : 32 * j + 32] for j in range(4)], 1))
    for side in range(2):
        cut = slice(side * LANES, (side + 1) * LANES)
        out[side, 0:32, :] = hi[:, cut].astype(F32)
        out[side, 32:64, :] = lo[:, cut].astype(F32)

    for copy in copies_zb:
        copy.wait_send()


def finish(g, d, conversion):
    first, twiddle, second = (jnp.asarray(table) for table in tables()[1:])
    vmem = pl.BlockSpec(memory_space=pltpu.VMEM)
    dma = pltpu.SemaphoreType.DMA
    return pl.pallas_call(
        finish_kernel,
        out_shape=(
            jax.ShapeDtypeStruct((2, 64, LANES), F32),
            jax.ShapeDtypeStruct((1, GRID_ROWS, DEGREES), BF16),
        ),
        in_specs=[vmem, vmem] + [pl.BlockSpec(memory_space=pltpu.HBM)] * 4,
        out_specs=(vmem, vmem),
        scratch_shapes=[
            pltpu.VMEM((NX, NY, 9, NZC, LANES), F32),
            pltpu.VMEM((NX, NY, 8, NZC, LANES), F32),
            pltpu.VMEM((2, NY, 9, NZC, LANES), F32),
            pltpu.VMEM((2, NX, 8, NZC, LANES), F32),
            pltpu.VMEM((2, 2, 9, NZC, LANES), F32),
            pltpu.VMEM((2, 2, 8, NZC, LANES), F32),
            pltpu.VMEM((2, 2, 9, NZC, LANES), F32),
            pltpu.VMEM((2, 2, 8, NZC, LANES), F32),
            pltpu.VMEM((NY, 9, NZC, LANES), F32),
            pltpu.VMEM((NX, 8, NZC, LANES), F32),
            pltpu.VMEM((3, 9, NZC, LANES), F32),
            pltpu.VMEM((3, 8, NZC, LANES), F32),
            pltpu.VMEM((24 * 8, LANES), F32),
            pltpu.VMEM((NZC, 16, LANES), F32),
            pltpu.VMEM((NZC, 8, LANES), F32),
            pltpu.VMEM((NZC, 16, LANES), F32),
            pltpu.VMEM((NZC, 8, LANES), F32),
            pltpu.VMEM((128, 256), BF16),
            pltpu.VMEM((2, 64, LANES), F32),
            pltpu.VMEM((128, 384), BF16),
            dma((7,)),
            dma((6,)), dma((6,)), dma((6,)), dma((6,)),
            dma((3,)), dma((3,)), dma((3,)), dma((3,)),
            dma((2, 7)), dma((2, 7)),
        ],
        compiler_params=pltpu.CompilerParams(
            collective_id=0, has_side_effects=True, vmem_limit_bytes=20 * MIB
        ),
        name="finish",
    )(g, d, *(pltpu.with_memory_space_constraint(operand, pltpu.HBM) for operand in (first, twiddle, second, conversion)))


def convert_kernel(spec, conv, out):
    total = jnp.zeros((4, DEGREES), F32)
    for block in range(16):
        here = pl.ds((block + 8) % 16, 4, stride=16)
        rows = jnp.concatenate([spec[0, here, :], spec[1, here, :]], 1).astype(BF16)
        part = conv[0, block * 256 : block * 256 + 256, :]
        total += jnp.dot(rows, part, preferred_element_type=F32)
    out[0] = total[0:2] + total[2:4]


def convert(spec, conversion):
    vmem = pl.BlockSpec(memory_space=pltpu.VMEM)
    return pl.pallas_call(
        convert_kernel,
        out_shape=jax.ShapeDtypeStruct((1, 2, DEGREES), F32),
        in_specs=[vmem, vmem],
        out_specs=vmem,
        compiler_params=pltpu.CompilerParams(vmem_limit_bytes=24 * MIB),
        name="convert",
    )(spec, conversion)


def shards(
    point_values, theta_weights, phi_weights, block_counts, theta_offsets, phi_offsets, conversion
):
    g, d = spread(point_values, theta_weights, phi_weights, block_counts, theta_offsets, phi_offsets)
    return convert(*finish(g, d, conversion))


def solution(mesh):
    placed = (
        P(None, ("lat", "lon"), None),
        P(("lat", "lon"), None, None),
        P(("lat", "lon"), None, None),
        P(("lat", "lon")),
        P(("lat", "lon")),
        P(("lat", "lon")),
        P(("lat", "lon"), None, None),
    )
    return jax.shard_map(
        shards, mesh=mesh, in_specs=placed, out_specs=P(("lat", "lon"), None, None), check_vma=False
    )
```

```python
import functools
import math

import jax
import jax.numpy as jnp
import numpy as np
from jax import lax
from jax.experimental import pallas as pl
from jax.experimental.pallas import tpu as pltpu
from jax.sharding import PartitionSpec as P

GRID_ROWS = 4096
GRID_COLS = 8192
ORDERS = 128
BLOCKS = 64
WIN_ROWS = 32
WIN_COLS = 128
PTS = 256
ROWS_DEV = 1024
COLS_DEV = 256
EXT_ROWS = ROWS_DEV + WIN_ROWS
EXT_COLS = COLS_DEV + WIN_COLS
DEGREES = 2048
LANES = 128
T0 = 64
T1 = ROWS_DEV // T0
NX, NY, NZC = 4, 4, 8
CHUNK = 16
NCHUNK = BLOCKS // CHUNK
G_ROWS = T1 * LANES + LANES
MESH = pl.DeviceIdType.MESH
MIB = 1 << 20
BF16 = jnp.bfloat16
F32 = jnp.float32


def split_np(table):
    hi = table.astype(jnp.bfloat16)
    lo = (table - hi.astype(np.float64)).astype(jnp.bfloat16)
    return hi, lo


@functools.cache
def tables():
    place = np.arange(ORDERS)
    gx, gy, zc = place // 32, place // 8 % 4, place % 8
    order = zc * 16 + gy * 4 + gx - ORDERS // 2
    phase = (order[:, None] * np.arange(EXT_COLS)[None, :]) % GRID_COLS * (2 * np.pi / GRID_COLS)
    base = np.concatenate([np.cos(phase), np.sin(phase)]).astype(np.float32)
    turn = (order[:, None] * np.arange(32)[None, :]) % 32 * (2 * np.pi / 32)
    rot = np.zeros((2 * ORDERS, LANES), np.float32)
    rot[:ORDERS, :32] = np.cos(turn)
    rot[:ORDERS, 32:64] = np.sin(turn)
    base = np.concatenate([base, rot], 1)

    index = np.arange(64)
    angle = index[:, None] * index[None, :] % 64 * (2 * np.pi / 64)
    cos, sin = np.cos(angle), np.sin(angle)
    hi, lo = split_np(np.concatenate([cos, sin]))
    first = np.concatenate([hi, lo, hi, np.zeros_like(hi)], 1)
    unitary = 1.0 / math.sqrt(GRID_ROWS * GRID_COLS)
    angle = index[:, None] * index[None, :] * (2 * np.pi / 4096)
    twiddle = np.stack([
        np.concatenate([np.cos(angle), np.cos(angle)], 1), np.concatenate([np.sin(angle), -np.sin(angle)], 1)
    ])
    twiddle = (twiddle * unitary).astype(np.float32)
    second = np.block([[cos, sin], [-sin, cos]]).reshape(2, 16, 4, 128).transpose(2, 0, 1, 3).reshape(128, 128)
    hi, lo = split_np(second)
    second = np.concatenate([hi, lo, hi], 1)
    return base, first, twiddle, second


def nt_dot(a, b):
    return lax.dot_general(a, b, (((1,), (1,)), ((), ())), preferred_element_type=F32)


def spread_kernel(
    counts_hbm, theta_offs_hbm, phi_offs_hbm, base_hbm, values_hbm, theta_hbm, phi_hbm, out, d,
    counts, theta_offs, phi_offs, base, values, theta, phi, win_a, win_b, ext, sems, small_sems,
):
    small = [
        pltpu.make_async_copy(source, dest, small_sems.at[k])
        for k, (source, dest) in enumerate((
            (base_hbm, base), (counts_hbm, counts), (values_hbm, values),
            (theta_offs_hbm, theta_offs), (phi_offs_hbm, phi_offs),
        ))
    ]
    for copy in small:
        copy.start()

    def fetch(c):
        part = pl.ds(c * CHUNK, CHUNK)
        return pltpu.make_async_copy(phi_hbm.at[part], phi.at[part], sems.at[0, c])

    def fetch_rows(k):
        part = (pl.ds(0, CHUNK), pl.ds(CHUNK, BLOCKS - CHUNK))[k]
        return pltpu.make_async_copy(theta_hbm.at[part], theta.at[part], sems.at[1, k])

    fetch_rows(0).start()
    fetch(0).start()
    fetch(1).start()
    fetch_rows(1).start()
    fetch(2).start()

    def clear(i, carry):
        for k in range(4):
            for x in range(2):
                ext[k, x, pl.ds(pl.multiple_of(i * 96, 8), 96), :] = jnp.zeros((96, LANES), F32)
        return carry

    lax.fori_loop(0, EXT_ROWS // 96, clear, 0)

    small[0].wait()
    lon = lax.axis_index("lon")
    place_of = lax.broadcasted_iota(jnp.int32, (ORDERS, LANES), 1)
    turn = base[:ORDERS, EXT_COLS:]
    turn_cos = jnp.sum(jnp.where(place_of == lon, turn, 0.0), axis=1, keepdims=True)
    turn_sin = jnp.sum(jnp.where(place_of == lon + 32, turn, 0.0), axis=1, keepdims=True)
    cos, sin = base[:ORDERS, :EXT_COLS], base[ORDERS:, :EXT_COLS]
    cos_hi, cos_lo = split(cos * turn_cos - sin * turn_sin)
    sin_hi, sin_lo = split(sin * turn_cos + cos * turn_sin)
    d[0:128, :] = cos_hi
    d[128:256, :] = sin_hi
    d[256:384, :] = cos_lo
    d[384:512, :] = sin_lo

    point = lax.broadcasted_iota(jnp.int32, (1, PTS), 1)
    lane = lax.broadcasted_iota(jnp.int32, (WIN_ROWS, LANES), 1)

    def windows(c, win):
        @pl.when(c + 3 < NCHUNK)
        def _():
            fetch(c + 3).start()

        fetch(c).wait()
        for n in range(CHUNK):
            b = c * CHUNK + n
            live = point < counts[b]
            rows = theta[b].astype(F32)
            parts = []
            for x in range(2):
                own = jnp.where(live, values[x, pl.ds(b, 1), :], 0.0)
                parts.append((rows * own).astype(BF16))
            win[n] = nt_dot(jnp.concatenate(parts, 0), phi[b])

    def place(c, win):
        for n in range(CHUNK):
            b = c * CHUNK + n
            row = theta_offs[b]
            col = phi_offs[b]
            tile = col // LANES
            shift = col % LANES
            near = lane >= shift
            here = pl.ds(row, WIN_ROWS)
            for x in range(2):
                moved = pltpu.roll(win[n, x * WIN_ROWS : (x + 1) * WIN_ROWS, :], shift, 1)
                ext[tile, x, here, :] += jnp.where(near, moved, 0.0)
                ext[tile + 1, x, here, :] += jnp.where(near, 0.0, moved)

    for copy in small[1:]:
        copy.wait()
    fetch_rows(0).wait()
    windows(0, win_a)
    fetch_rows(1).wait()

    def step(i, carry):
        windows(2 * i + 1, win_b)
        place(2 * i, win_a)
        windows(2 * i + 2, win_a)
        place(2 * i + 1, win_b)
        return carry

    lax.fori_loop(0, NCHUNK // 2 - 1, step, 0)
    windows(NCHUNK - 1, win_b)
    place(NCHUNK - 2, win_a)
    place(NCHUNK - 1, win_b)

    for k in range(3):
        cols = slice(k * LANES, (k + 1) * LANES)
        for x in range(2):
            for t1 in range(T1):
                at = t1 * LANES + x * T0
                out[at : at + T0, cols] = ext[k, x, t1 * T0 : (t1 + 1) * T0, :].astype(BF16)
            at = T1 * LANES + x * T0
            out[at : at + 32, cols] = ext[k, x, ROWS_DEV:EXT_ROWS, :].astype(BF16)
            out[at + 32 : at + 64, cols] = jnp.zeros((32, LANES), BF16)


def spread(point_values, theta_weights, phi_weights, block_counts, theta_offsets, phi_offsets):
    base = jnp.asarray(tables()[0])
    vmem = pl.BlockSpec(memory_space=pltpu.VMEM)
    operands = [block_counts, theta_offsets, phi_offsets, base, point_values, theta_weights, phi_weights]
    return pl.pallas_call(
        spread_kernel,
        out_shape=(
            jax.ShapeDtypeStruct((G_ROWS, EXT_COLS), BF16),
            jax.ShapeDtypeStruct((4 * ORDERS, EXT_COLS), BF16),
        ),
        in_specs=[pl.BlockSpec(memory_space=pltpu.HBM)] * len(operands),
        out_specs=(vmem, vmem),
        scratch_shapes=[
            pltpu.SMEM((BLOCKS,), jnp.int32),
            pltpu.SMEM((BLOCKS,), jnp.int32),
            pltpu.SMEM((BLOCKS,), jnp.int32),
            pltpu.VMEM((2 * ORDERS, EXT_COLS + LANES), F32),
            pltpu.VMEM((2, BLOCKS, PTS), F32),
            pltpu.VMEM((BLOCKS, WIN_ROWS, PTS), BF16),
            pltpu.VMEM((BLOCKS, WIN_COLS, PTS), BF16),
            pltpu.VMEM((CHUNK, 2 * WIN_ROWS, WIN_COLS), F32),
            pltpu.VMEM((CHUNK, 2 * WIN_ROWS, WIN_COLS), F32),
            pltpu.VMEM((4, 2, EXT_ROWS, LANES), F32),
            pltpu.SemaphoreType.DMA((2, NCHUNK)),
            pltpu.SemaphoreType.DMA((5,)),
        ],
        compiler_params=pltpu.CompilerParams(vmem_limit_bytes=24 * MIB),
        name="spread",
    )(*(pltpu.with_memory_space_constraint(operand, pltpu.HBM) for operand in operands))


def split(value):
    hi = value.astype(BF16)
    return hi, (value - hi.astype(F32)).astype(BF16)


def finish_kernel(
    g, d, first_hbm, twiddle_hbm, second_hbm, conv_hbm, out, conv,
    a, b, got_a, got_b, relay_a, relay_b, on_a, on_b, sum_a, sum_b, got_a2, got_b2,
    q, qz_a, qz_b, r_a, r_b, first, twiddle, second,
    conv_sem, send_a, recv_a, send_b, recv_b, send_a2, recv_a2, send_b2, recv_b2, send_z, recv_z,
):
    lat = lax.axis_index("lat")
    lon = lax.axis_index("lon")
    z_lo = lon // 16
    my = lon // 4 % 4
    mx = lon % 4
    zc = lat * 2 + z_lo

    def x_peer(by):
        to = lax.rem(mx + by, NX)
        return to, (lat, z_lo * 16 + my * 4 + to)

    def y_peer(by):
        to = lax.rem(my + by, NY)
        return to, (lat, z_lo * 16 + to * 4 + mx)

    def z_peer(by):
        to = lax.rem(zc + by, NZC)
        return to, (to // 2, to % 2 * 16 + my * 4 + mx)

    barrier = pltpu.get_barrier_semaphore()
    far_first = [(z_peer, by) for by in (4, 3, 5, 1, 7, 2, 6)] + [(peer, by) for by in (2, 1, 3) for peer in (x_peer, y_peer)]
    for peer, by in far_first:
        pl.semaphore_signal(barrier, inc=1, device_id=peer(by)[1], device_id_type=MESH)

    half = T1 * LANES // 2
    conv_loads = [
        pltpu.make_async_copy(conv_hbm, conv, conv_sem.at[k])
        for k in range(1)
    ]
    table_loads = [
        pltpu.make_async_copy(source, dest, conv_sem.at[4 + k])
        for k, (source, dest) in enumerate(((first_hbm, first), (twiddle_hbm, twiddle), (second_hbm, second)))
    ]
    for copy in table_loads:
        copy.start()
    for copy in conv_loads:
        copy.start()

    early = lax.broadcasted_iota(jnp.int32, (ORDERS, LANES), 1) < 64

    def along(product, at):
        cut = slice(at * LANES, (at + 1) * LANES)
        by_cos = product[0:128, cut] + product[256:384, cut]
        by_sin = pltpu.roll(product[128:256, cut] + product[384:512, cut], 64, 1)
        return (by_cos + jnp.where(early, by_sin, -by_sin)).reshape(NX, NY, NZC, LANES)

    for pair in range(4):
        product = nt_dot(d[...], g[pair * 256 : pair * 256 + 256, :])
        for at in range(2):
            a[:, :, pair * 2 + at, :, :] = along(product, at)
    for pair in range(4):
        product = nt_dot(d[...], g[half + pair * 256 : half + pair * 256 + 256, :])
        for at in range(2):
            b[:, :, pair * 2 + at, :, :] = along(product, at)
    a[:, :, 8, :, :] = along(nt_dot(d[...], g[T1 * LANES : G_ROWS, :]), 0)
    pl.semaphore_wait(barrier, (NX - 1) + (NY - 1) + (NZC - 1))

    def ring(part, peer, relay, on, got, send, recv):
        (ahead, ahead_id), (across, _), (behind, behind_id) = peer(1), peer(2), peer(3)

        def copy(k, source, dest, device):
            return pltpu.make_async_remote_copy(
                src_ref=source, dst_ref=dest, send_sem=send.at[k], recv_sem=recv.at[k],
                device_id=device, device_id_type=MESH,
            )

        low, high = pl.ds(0, 2), pl.ds(2, 2)
        copies = [
            copy(0, part(across, low), relay.at[0], ahead_id),
            copy(1, part(across, high), relay.at[1], behind_id),
            copy(2, part(ahead, high), got.at[0, high], ahead_id),
            copy(3, part(behind, low), got.at[1, low], behind_id),
            copy(4, on.at[0], got.at[0, low], ahead_id),
            copy(5, on.at[1], got.at[1, high], behind_id),
        ]
        def pass_on():
            copies[0].wait_recv()
            on[0] = part(ahead, low)[...] + relay[0]
            copies[4].start()
            copies[1].wait_recv()
            on[1] = part(behind, high)[...] + relay[1]
            copies[5].start()

        return copies, pass_on

    copies_a, pass_on_a = ring(lambda to, side: a.at[to, side], x_peer, relay_a, on_a, got_a, send_a, recv_a)
    copies_b, pass_on_b = ring(lambda to, side: b.at[side, to], y_peer, relay_b, on_b, got_b, send_b, recv_b)
    for one in copies_a[:2] + copies_b[:2] + copies_a[2:4] + copies_b[2:4]:
        one.start()
    pass_on_a()
    pass_on_b()

    def exchange(source, dest, peer, send, recv):
        copies = []
        for by in (2, 1, 3):
            to, device = peer(by)
            copies.append(pltpu.make_async_remote_copy(
                src_ref=source.at[to], dst_ref=dest.at[by - 1], send_sem=send.at[by - 1], recv_sem=recv.at[by - 1],
                device_id=device, device_id_type=MESH,
            ))
        for copy in copies:
            copy.start()
        return copies

    for copy in copies_a[2:]:
        copy.wait_recv()
    sum_a[...] = a[mx] + got_a[0] + got_a[1]
    copies_a2 = exchange(sum_a, got_a2, y_peer, send_a2, recv_a2)
    for copy in copies_b[2:]:
        copy.wait_recv()
    sum_b[...] = b[:, my] + got_b[0] + got_b[1]
    copies_b2 = exchange(sum_b, got_b2, x_peer, send_b2, recv_b2)

    def deliver(source, dest, row):
        copies = []
        for by in (4, 3, 5, 1, 7, 2, 6):
            to, device = z_peer(by)
            copies.append(pltpu.make_async_remote_copy(
                src_ref=source.at[to], dst_ref=dest.at[zc],
                send_sem=send_z.at[row, by - 1], recv_sem=recv_z.at[row, by - 1],
                device_id=device, device_id_type=MESH,
            ))
        for copy in copies:
            copy.start()
        dest[zc] = source[zc]
        return copies

    q[72:128, :] = jnp.zeros((56, LANES), F32)
    out[:, 64:128, :] = jnp.zeros((2, 64, LANES), F32)
    for copy in copies_a2:
        copy.wait_recv()
    q[0:72, :] = ((sum_a[my] + got_a2[0]) + (got_a2[1] + got_a2[2])).reshape(72, LANES)
    for z in range(NZC):
        qz_a[z] = q[pl.ds(z, 16, stride=8), :]
    copies_za = deliver(qz_a, r_a, 0)
    for copy in copies_b2:
        copy.wait_recv()
    q[128:192, :] = ((sum_b[mx] + got_b2[0]) + (got_b2[1] + got_b2[2])).reshape(64, LANES)
    for z in range(NZC):
        qz_b[z] = q[pl.ds(128 + z, 8, stride=8), :]
    copies_zb = deliver(qz_b, r_b, 1)
    for group in (copies_a, copies_b, copies_a2, copies_b2, copies_za):
        for copy in group:
            copy.wait_send()
    for copy in table_loads + conv_loads:
        copy.wait()
    for copy in copies_za + copies_zb:
        copy.wait_recv()

    first_rows = [r_a[2 * i] + r_a[2 * i + 1] for i in range(4)]
    top = lax.broadcasted_iota(jnp.int32, (T1, LANES), 0) == 0
    rows = [
        jnp.concatenate([first_rows[i][0:8, :], r_b[2 * i] + r_b[2 * i + 1]], 0)
        + jnp.where(top, jnp.broadcast_to(first_rows[i - 1][8:9, :], (T1, LANES)), 0.0)
        for i in range(4)
    ]
    hi, lo = split(jnp.concatenate(rows, 0))
    both = jnp.dot(first[...], jnp.concatenate([hi, hi, lo, jnp.zeros_like(hi)], 0), preferred_element_type=F32)
    by_sin = pltpu.roll(both[64:128], 64, 1)
    inner = both[0:64] + jnp.where(early[0:64], by_sin, -by_sin)
    turned = inner * twiddle[0] + pltpu.roll(inner, 64, 1) * twiddle[1]
    hi, lo = split(turned)
    parts = nt_dot(second[...], jnp.concatenate([hi, hi, lo], 1))
    hi, lo = split(jnp.concatenate([parts[32 * j : 32 * j + 32] for j in range(4)], 1))
    for side in range(2):
        cut = slice(side * LANES, (side + 1) * LANES)
        out[side, 0:32, :] = hi[:, cut].astype(F32)
        out[side, 32:64, :] = lo[:, cut].astype(F32)

    for copy in copies_zb:
        copy.wait_send()


def finish(g, d, conversion):
    first, twiddle, second = (jnp.asarray(table) for table in tables()[1:])
    vmem = pl.BlockSpec(memory_space=pltpu.VMEM)
    dma = pltpu.SemaphoreType.DMA
    return pl.pallas_call(
        finish_kernel,
        out_shape=(
            jax.ShapeDtypeStruct((2, 128, LANES), F32),
            jax.ShapeDtypeStruct((1, GRID_ROWS, DEGREES), BF16),
        ),
        in_specs=[vmem, vmem] + [pl.BlockSpec(memory_space=pltpu.HBM)] * 4,
        out_specs=(vmem, vmem),
        scratch_shapes=[
            pltpu.VMEM((NX, NY, 9, NZC, LANES), F32),
            pltpu.VMEM((NX, NY, 8, NZC, LANES), F32),
            pltpu.VMEM((2, NY, 9, NZC, LANES), F32),
            pltpu.VMEM((2, NX, 8, NZC, LANES), F32),
            pltpu.VMEM((2, 2, 9, NZC, LANES), F32),
            pltpu.VMEM((2, 2, 8, NZC, LANES), F32),
            pltpu.VMEM((2, 2, 9, NZC, LANES), F32),
            pltpu.VMEM((2, 2, 8, NZC, LANES), F32),
            pltpu.VMEM((NY, 9, NZC, LANES), F32),
            pltpu.VMEM((NX, 8, NZC, LANES), F32),
            pltpu.VMEM((3, 9, NZC, LANES), F32),
            pltpu.VMEM((3, 8, NZC, LANES), F32),
            pltpu.VMEM((24 * 8, LANES), F32),
            pltpu.VMEM((NZC, 16, LANES), F32),
            pltpu.VMEM((NZC, 8, LANES), F32),
            pltpu.VMEM((NZC, 16, LANES), F32),
            pltpu.VMEM((NZC, 8, LANES), F32),
            pltpu.VMEM((128, 256), BF16),
            pltpu.VMEM((2, 64, LANES), F32),
            pltpu.VMEM((128, 384), BF16),
            dma((7,)),
            dma((6,)), dma((6,)), dma((6,)), dma((6,)),
            dma((3,)), dma((3,)), dma((3,)), dma((3,)),
            dma((2, 7)), dma((2, 7)),
        ],
        compiler_params=pltpu.CompilerParams(
            collective_id=0, has_side_effects=True, vmem_limit_bytes=20 * MIB
        ),
        name="finish",
    )(g, d, *(pltpu.with_memory_space_constraint(operand, pltpu.HBM) for operand in (first, twiddle, second, conversion)))


def convert_kernel(spec, conv, out):
    total = jnp.zeros((8, DEGREES), F32)
    for block in range(16):
        here = pl.ds((block + 8) % 16, 8, stride=16)
        rows = jnp.concatenate([spec[0, here, :], spec[1, here, :]], 1).astype(BF16)
        part = conv[0, block * 256 : block * 256 + 256, :]
        total += jnp.dot(rows, part, preferred_element_type=F32)
    out[0] = total[0:2] + total[2:4]


def convert(spec, conversion):
    vmem = pl.BlockSpec(memory_space=pltpu.VMEM)
    return pl.pallas_call(
        convert_kernel,
        out_shape=jax.ShapeDtypeStruct((1, 2, DEGREES), F32),
        in_specs=[vmem, vmem],
        out_specs=vmem,
        compiler_params=pltpu.CompilerParams(vmem_limit_bytes=24 * MIB),
        name="convert",
    )(spec, conversion)


def shards(
    point_values, theta_weights, phi_weights, block_counts, theta_offsets, phi_offsets, conversion
):
    g, d = spread(point_values, theta_weights, phi_weights, block_counts, theta_offsets, phi_offsets)
    return convert(*finish(g, d, conversion))


def solution(mesh):
    placed = (
        P(None, ("lat", "lon"), None),
        P(("lat", "lon"), None, None),
        P(("lat", "lon"), None, None),
        P(("lat", "lon")),
        P(("lat", "lon")),
        P(("lat", "lon")),
        P(("lat", "lon"), None, None),
    )
    return jax.shard_map(
        shards, mesh=mesh, in_specs=placed, out_specs=P(("lat", "lon"), None, None), check_vma=False
    )
```
